512 devices in a mesh: dp: 64 (over y_hi, z, core), tensor: 8 (over x, y_lo).
Axes of the slice: x: 4, y: 4 (y_hi: 2, y_lo: 2; y = y_hi * 2 + y_lo), z: 16, core: 2. Of those that a mesh axis runs over, the one named last changes fastest.
Arguments:
- inputs: bfloat16 [16384, 2560], P('dp', 'tensor'), may hold values from -37 to 37
- gate_values: bfloat16 [16384, 8192], P('dp', 'tensor'), may hold values from -8 to 8
- up_values: bfloat16 [16384, 8192], P('dp', 'tensor'), may hold values from -6 to 6
- hidden_cotangent: bfloat16 [16384, 8192], P('dp', 'tensor'), may hold values from -37 to 37
- owners: int32 [8, 16], P('tensor'), may hold values from 0 to 15, each once within a row
- left_inverse: float32 [64, 8, 320, 320], P('dp', 'tensor'), may hold values from -2 to 16, as said below
- right_inverse: float32 [64, 8, 512, 128], P('dp', 'tensor'), may hold values from -2 to 16, as said below
Outputs:
- input_factor: float32 [8, 320, 320], P('tensor', 'dp')
- output_factor: float32 [8, 1024, 512], P('tensor', 'dp')
- preconditioned: float32 [8, 320, 8192], P(None, 'dp', 'tensor')
The draws below stay inside these ranges and needn't reach their ends.
Inputs may be any that keep to these rules, and one draw needn't show every extreme that they name: `owners`: each row is an ordering of the 16 worker groups. `left_inverse`: diagonal entries lie in 4 to 16. `right_inverse`: block [i, t] is columns (i % 4) * 128 onward of a matrix whose diagonal entries lie in 4 to 16.
All inputs are finite; a program needn't handle non-finite values.
Results may differ from the reference program's by a relative error of at most 0.0029.
Values may be sent and summed in bfloat16 or wider, within the bound.
A program may use at most 128 MiB of HBM per device.

```python
import math
import jax
import jax.numpy as jnp
from jax import lax

FEAT = 2560
HID = 8192
BLOCK_OUT = 512
TOKENS = 16384
BLOCK_IN = 320
HID_DEV = 1024
COL_BLOCKS = 2
TILES = 16
WORKERS = 4
COL_PIECE = 128
N_DP = 64
N_TENSOR = 8


def rise_scales(key, rows, cols):
    key_rows, key_cols = jax.random.split(key)
    rising = 0.5 + jnp.arange(rows, dtype=jnp.float32) / rows
    row_part = jnp.exp(jax.random.uniform(key_rows, (rows,), jnp.float32, -0.7, 0.7))
    col_part = jnp.exp(jax.random.uniform(key_cols, (cols,), jnp.float32, -0.7, 0.7))
    return (rising * row_part)[:, None] * col_part[None, :]


def draw_inputs(key, part):
    key = jax.random.fold_in(key, 11)
    key_base, key_scale = jax.random.split(key)
    base = jnp.clip(jax.random.normal(key_base, (TOKENS, FEAT), jnp.float32), -6.0, 6.0)
    return (base * rise_scales(key_scale, TOKENS, FEAT)).astype(jnp.bfloat16)


def draw_hidden_cotangent(key, part):
    key = jax.random.fold_in(key, 12)
    key_base, key_scale = jax.random.split(key)
    base = jnp.clip(jax.random.normal(key_base, (TOKENS, HID), jnp.float32), -6.0, 6.0)
    return (base * rise_scales(key_scale, TOKENS, HID)).astype(jnp.bfloat16)


def draw_left_inverse(key, part):
    key = jax.random.fold_in(key, 13)
    key_diag, key_rest = jax.random.split(key)
    shape = (N_DP, N_TENSOR, BLOCK_IN, BLOCK_IN)
    spread_part = jnp.clip(jax.random.normal(key_rest, shape, jnp.float32), -6.0, 6.0)
    diagonal = jnp.exp(jax.random.uniform(key_diag, shape[:-1], jnp.float32, math.log(4.0), math.log(16.0)))
    identity = jnp.eye(BLOCK_IN, dtype=jnp.float32)
    return spread_part * (2.5 / math.sqrt(BLOCK_IN)) * (1.0 - identity) + diagonal[..., None] * identity


def draw_right_inverse(key, part):
    key = jax.random.fold_in(key, 14)
    key_diag, key_rest = jax.random.split(key)
    shape = (N_DP, N_TENSOR, BLOCK_OUT, COL_PIECE)
    spread_part = jnp.clip(jax.random.normal(key_rest, shape, jnp.float32), -6.0, 6.0)
    diagonal = jnp.exp(jax.random.uniform(key_diag, (N_DP, N_TENSOR, 1, COL_PIECE), jnp.float32, math.log(4.0), math.log(16.0)))
    first = jnp.arange(N_DP, dtype=jnp.int32) % WORKERS * COL_PIECE
    rows = jnp.arange(BLOCK_OUT, dtype=jnp.int32)
    cols = jnp.arange(COL_PIECE, dtype=jnp.int32)
    marks = (rows[None, :, None] == first[:, None, None] + cols[None, None, :]).astype(jnp.float32)
    marks = marks[:, None, :, :]
    return spread_part * (2.5 / math.sqrt(BLOCK_OUT)) * (1.0 - marks) + diagonal * marks


def shard_levels(key, shape, cuts, least, largest):
    factor_of = 1.0
    for position, blocks in cuts:
        draws = jax.random.uniform(jax.random.fold_in(jax.random.fold_in(key, 6), position), (blocks,), jnp.float32, least / len(cuts), largest / len(cuts))
        factor_of = factor_of * jnp.repeat(jnp.exp(draws), shape[position] // blocks).reshape((-1,) + (1,) * (len(shape) - 1 - position))
    return factor_of


def centred(stream_key, shape, deviation, limit, pieces=(), kind=jnp.bfloat16):
    array = jax.random.normal(stream_key, shape, jnp.float32) * deviation
    if len(pieces) > 0:
        array = shard_levels(stream_key, shape, pieces, -0.22, 0.18) * array
    return jnp.clip(array, min=-limit, max=limit).astype(kind)


def setup_inputs(seed: int = 0) -> dict:
    streams_of = jax.random.split(jax.random.key(seed), 8)
    return {
        "inputs": draw_inputs(jax.random.fold_in(streams_of[7], 71), 0),
        "gate_values": centred(streams_of[1], (TOKENS, HID), 1.5, 8.0, ((0, 64), (1, 8))),
        "up_values": centred(streams_of[2], (TOKENS, HID), 1.0, 6.0, ((0, 64), (1, 8))),
        "hidden_cotangent": draw_hidden_cotangent(jax.random.fold_in(streams_of[7], 71), 0),
        "owners": jax.vmap(lambda own: jax.random.permutation(own, TILES))(jax.random.split(streams_of[4], N_TENSOR)).reshape((N_TENSOR, TILES)).astype(jnp.int32),
        "left_inverse": draw_left_inverse(jax.random.fold_in(streams_of[7], 71), 0),
        "right_inverse": draw_right_inverse(jax.random.fold_in(streams_of[7], 71), 0),
    }


HIGHEST = lax.Precision.HIGHEST


def gate_gradient(gate_values, up_values, hidden_cotangent):
    pre_act = gate_values.astype(jnp.float32)
    sigma = jax.nn.sigmoid(pre_act)
    slope = sigma * (1.0 + pre_act * (1.0 - sigma))
    return (hidden_cotangent.astype(jnp.float32) * up_values.astype(jnp.float32) * slope).astype(jnp.bfloat16)


def reference(inputs, gate_values, up_values, hidden_cotangent, owners, left_inverse, right_inverse):
    gate_grad = gate_gradient(gate_values, up_values, hidden_cotangent)
    wide_inputs = inputs.astype(jnp.float32).reshape(TOKENS, N_TENSOR, BLOCK_IN)
    input_factor = jnp.einsum("nar,nas->ars", wide_inputs, wide_inputs, precision=HIGHEST) / TOKENS
    groups = gate_grad.reshape(TOKENS, N_TENSOR, HID_DEV).transpose(1, 0, 2)
    left_groups = left_inverse.transpose(1, 0, 2, 3)
    right_groups = right_inverse.transpose(1, 0, 2, 3)
    worker_ids = jnp.arange(WORKERS, dtype=jnp.int32)

    def per_group(operands):
        group_grad, owner_row, left_group, right_group = operands
        blocks = group_grad.astype(jnp.float32).reshape(TOKENS, COL_BLOCKS, BLOCK_OUT)
        out_blocks = jnp.einsum("nci,ncj->cij", blocks, blocks, precision=HIGHEST) / TOKENS
        weight_grad = jnp.dot(inputs.T, group_grad, preferred_element_type=jnp.float32) / TOKENS
        tiles = weight_grad.reshape(N_TENSOR, BLOCK_IN, COL_BLOCKS, BLOCK_OUT).transpose(0, 2, 1, 3)
        tiles = tiles.reshape(TILES, BLOCK_IN, BLOCK_OUT)
        devices = (owner_row.astype(jnp.int32)[:, None] * WORKERS + worker_ids[None, :]).reshape(-1)
        left_sel = jnp.take(left_group, devices, axis=0).reshape(TILES, WORKERS, BLOCK_IN, BLOCK_IN)
        right_sel = jnp.take(right_group, devices, axis=0).reshape(TILES, WORKERS, BLOCK_OUT, COL_PIECE)
        right_part = jnp.einsum("kab,kwbc->kwac", tiles, right_sel, precision=HIGHEST)
        finished = jnp.einsum("kwra,kwac->kwrc", left_sel, right_part, precision=HIGHEST)
        placed = finished.reshape(N_TENSOR, COL_BLOCKS, WORKERS, BLOCK_IN, COL_PIECE).transpose(0, 3, 1, 2, 4)
        return out_blocks.reshape(HID_DEV, BLOCK_OUT), placed.reshape(N_TENSOR, BLOCK_IN, HID_DEV)

    output_factor, placed = lax.map(per_group, (groups, owners, left_groups, right_groups))
    preconditioned = placed.transpose(1, 2, 0, 3).reshape(N_TENSOR, BLOCK_IN, HID)
    return input_factor, output_factor, preconditioned
```

```python
import jax
import jax.numpy as jnp
import numpy as np
from jax import lax
from jax.experimental import pallas as pl
from jax.experimental.pallas import tpu as pltpu
from jax.sharding import PartitionSpec as P

MESH = pl.DeviceIdType.MESH
HIGHEST = lax.Precision.HIGHEST
F32 = jnp.float32
BF16 = jnp.bfloat16
Z = 16
HOPS = 8
NARROW = 4
TOTAL = 16384
STREAM_ROWS = (48, 80, 80)


def kernel(
    gate_ref, up_ref, cot_ref, xt_ref, sel_ref, left_ref, right_ref, pick_ref, owner_ref,
    input_ref, output_ref, pre_ref,
    xb, ib, gb, osum, isum, part, tile, fin, ret,
    rb0, rf0, sb0, sf0, rb1, rf1, sb1, sf1, rb2, rf2, sb2, sf2,
    y_s, y_r, x_s, x_r, cx_s, cx_r, gy_s, gy_r, gc_s, gc_r, rs_s, rs_r, d_s, d_r, dc_s, dc_r, t_s, t_r,
):
    dp = lax.axis_index("dp")
    tn = lax.axis_index("tensor")
    h, z, c = dp // 32, (dp // 2) % Z, dp % 2
    x, ylo = tn // 2, tn % 2
    y = h * 2 + ylo

    def dev(x_, y_, z_, c_):
        return ((y_ // 2) * 32 + z_ * 2 + c_, x_ * 2 + y_ % 2)

    xr, xl = (x + 1) % 4, (x + 3) % 4
    zr, zl = (z + 1) % Z, (z + Z - 1) % Z
    zx = z + 1 - 2 * (z % 2)
    sibling = dev(x, y, z, 1 - c)
    across = dev(x, (y + 2) % 4, z, c)
    right, left = dev(xr, y, z, c), dev(xl, y, z, c)
    up_z, down_z = dev(x, y, zr, c), dev(x, y, zl, c)
    diagonal = dev(x, (y + 2) % 4, zx, c)
    ring_y = [dev(x, (y + k) % 4, z, c) for k in (1, 2, 3)]

    barrier = pltpu.get_barrier_semaphore()
    peers = ring_y + [right, left, sibling, up_z, down_z, diagonal]
    for peer in peers:
        pl.semaphore_signal(barrier, inc=1, device_id=peer, device_id_type=MESH)
    pl.semaphore_wait(barrier, len(peers))

    sends = []

    def send(src, dst, s_sem, r_sem, to):
        copy = pltpu.make_async_remote_copy(
            src_ref=src, dst_ref=dst, send_sem=s_sem, recv_sem=r_sem, device_id=to, device_id_type=MESH
        )
        copy.start()
        sends.append(copy)

    def arrive(dst, s_sem, r_sem):
        pltpu.make_async_remote_copy(
            src_ref=dst, dst_ref=dst, send_sem=s_sem, recv_sem=r_sem, device_id=sibling, device_id_type=MESH
        ).wait_recv()

    for k in (1, 3):
        half = ((y + k) % 4) // 2
        send(xt_ref.at[half], xb.at[c, x, y], y_s.at[k], y_r.at[k], ring_y[k - 1])
    send(xt_ref, ib.at[c, h], y_s.at[2], y_r.at[2], across)
    xb[c, x, y] = xt_ref[h]
    ib[c, h] = xt_ref[...]

    for n in range(4):
        cols = slice(n * 256, n * 256 + 256)
        pre = gate_ref[:, cols].astype(F32)
        s = jax.nn.sigmoid(pre)
        slope = s * (1.0 + pre * (1.0 - s))
        gb[c, h, n] = (cot_ref[:, cols].astype(F32) * up_ref[:, cols].astype(F32) * slope).astype(BF16)
        mine = gb.at[c, h, n]
        send(mine, mine, gy_s.at[n], gy_r.at[n], across)
        send(mine, mine, gc_s.at[n], gc_r.at[n], sibling)

    for k in (1, 3):
        arrive(xb.at[c, x, (y + 4 - k) % 4], y_s.at[k], y_r.at[k])
    arrive(ib.at[c, 1 - h], y_s.at[2], y_r.at[2])
    xb[c, x, (y + 2) % 4] = ib[c, 1 - h, h]
    own = xb.at[c, x]
    send(own, own, x_s.at[0], x_r.at[0], right)
    send(own, own, x_s.at[1], x_r.at[1], left)
    send(own, own, cx_s.at[0], cx_r.at[0], sibling)
    send(ib.at[c], ib.at[c], cx_s.at[4], cx_r.at[4], sibling)

    from_l, from_r, far = xb.at[c, xl], xb.at[c, xr], (x + 2) % 4
    arrive(from_l, x_s.at[0], x_r.at[0])
    low = xb.at[c, xl, pl.ds(0, 2)]
    send(low, low, x_s.at[2], x_r.at[2], right)
    arrive(from_r, x_s.at[1], x_r.at[1])
    high = xb.at[c, xr, pl.ds(2, 2)]
    send(high, high, x_s.at[3], x_r.at[3], left)
    send(from_l, from_l, cx_s.at[1], cx_r.at[1], sibling)
    send(from_r, from_r, cx_s.at[2], cx_r.at[2], sibling)

    for n in range(4):
        other = gb.at[c, 1 - h, n]
        arrive(other, gy_s.at[n], gy_r.at[n])
        send(other, other, gc_s.at[4 + n], gc_r.at[4 + n], sibling)
    for n in range(4):
        arrive(gb.at[1 - c, h, n], gc_s.at[n], gc_r.at[n])
    for n in range(4):
        arrive(gb.at[1 - c, 1 - h, n], gc_s.at[4 + n], gc_r.at[4 + n])
    arrive(ib.at[1 - c], cx_s.at[4], cx_r.at[4])

    for i in range(2):
        for j in range(2):
            total = jnp.zeros((256, 256), F32)
            for k in range(2):
                for m in range(2):
                    total += lax.dot_general(
                        gb[k, m, 2 * h + i], gb[k, m, 2 * h + j],
                        (((0,), (0,)), ((), ())), preferred_element_type=F32,
                    )
            osum[pl.ds(i * 256, 256), pl.ds(j * 256, 256)] = total
    isum[...] = jnp.zeros_like(isum)
    for half in range(2):
        total = jnp.zeros((256, 160), F32)
        for k in range(2):
            for m in range(2):
                rows = jnp.dot(sel_ref[...], ib[k, m, h], preferred_element_type=F32).astype(BF16)
                total += lax.dot_general(
                    rows, ib[k, m, half], (((1,), (1,)), ((), ())), preferred_element_type=F32
                )
        isum[:, half * 160:half * 160 + 160] = total

    arrive(xb.at[c, far, pl.ds(0, 2)], x_s.at[2], x_r.at[2])
    arrive(xb.at[c, far, pl.ds(2, 2)], x_s.at[3], x_r.at[3])
    send(xb.at[c, far], xb.at[c, far], cx_s.at[3], cx_r.at[3], sibling)
    for k, p in enumerate((x, xl, xr, far)):
        arrive(xb.at[1 - c, p], cx_s.at[k], cx_r.at[k])

    def partial_tile(t, slot):
        px, py, pc = pick_ref[0, t], pick_ref[1, t], pick_ref[2, t]
        total = jnp.zeros((160, 256), F32)
        for k in range(2):
            for m in range(2):
                total += jnp.dot(xb[k, px, 2 * m + py], gb[k, m, 2 * pc + c], preferred_element_type=F32)
        part[slot] = total

    def factor_rows(t):
        o_rows = pl.ds(pl.multiple_of(t * 32 + c * 16, 16), 16)
        i_rows = pl.ds(pl.multiple_of(t * 16 + c * 8, 8), 8)
        return jnp.concatenate(
            [osum[o_rows, 0:256], osum[o_rows, 256:512], isum[i_rows, 0:256], isum[i_rows, 256:512]], axis=0
        )

    bufs = ((rb0, rf0, sb0, sf0), (rb1, rf1, sb1, sf1), (rb2, rf2, sb2, sf2))

    def own_part(stream, t, slot):
        if stream == 0:
            return factor_rows(t)
        return part[slot, (stream - 1) * 80:(stream - 1) * 80 + 80]

    def landing(stream, way, step):
        rb, rf = bufs[stream][:2]
        return rb.at[way, step] if step < NARROW else rf.at[way, step - NARROW]

    def hop(stream, way, step, t, slot):
        value = own_part(stream, t, slot)
        if step > 0:
            came = landing(stream, way, step - 1)
            arrive(came, rs_s.at[stream, way, step - 1], rs_r.at[stream, way, step - 1])
            value = value + came[...].astype(F32)
        sb, sf = bufs[stream][2:]
        out = sb.at[way, step] if step < NARROW else sf.at[way, step - NARROW]
        out[...] = value.astype(out.dtype)
        send(out, landing(stream, way, step), rs_s.at[stream, way, step], rs_r.at[stream, way, step],
             up_z if way == 0 else down_z)

    def target(way, step):
        return (z + 7 - step) % Z if way == 0 else (z + 8 + step) % Z

    lengths = (7, 8)
    for step in range(HOPS):
        for way in range(2):
            if step < lengths[way]:
                partial_tile(target(way, step), (step % 2) * 2 + way)
        for stream in range(3):
            for way in range(2):
                if step < lengths[way]:
                    hop(stream, way, step, target(way, step), (step % 2) * 2 + way)
    partial_tile(z, 0)

    def finish(stream):
        value = own_part(stream, z, 0)
        for way in range(2):
            last = lengths[way] - 1
            came = landing(stream, way, last)
            arrive(came, rs_s.at[stream, way, last], rs_r.at[stream, way, last])
            value = value + came[...].astype(F32)
        return value * (1.0 / TOTAL)

    factors = finish(0)
    output_ref[:, 0:256] = factors[0:16]
    output_ref[:, 256:512] = factors[16:32]
    input_ref[:, 0:256] = factors[32:37]
    input_ref[:, 256:320] = factors[40:45, 0:64]

    goes = z % 2
    stays = h == goes
    done = sb_tile = tile.at[2]
    done[c, 0:80] = finish(1).astype(BF16)
    done[c, 80:160] = finish(2).astype(BF16)
    mine = tile.at[2, c]
    send(mine, tile.at[h, c], d_s.at[0], d_r.at[h], dev(x, goes * 2 + ylo, zx, c))

    @pl.when(stays)
    def _():
        tile[h, c] = tile[2, c]

    @pl.when(jnp.logical_not(stays))
    def _():
        pltpu.make_async_remote_copy(
            src_ref=mine, dst_ref=tile.at[h, c], send_sem=d_s.at[1], recv_sem=d_r.at[h],
            device_id=across, device_id_type=MESH,
        ).start()
        arrive(tile.at[h, c], d_s.at[0], d_r.at[h])

    arrive(tile.at[1 - h, c], d_s.at[0], d_r.at[1 - h])
    for k in range(2):
        send(tile.at[k, c], tile.at[k, c], dc_s.at[k], dc_r.at[k], sibling)
    for k in range(2):
        arrive(tile.at[k, 1 - c], dc_s.at[k], dc_r.at[k])

    right_all = right_ref[...]
    right_hi = right_all.astype(BF16)
    right_lo = (right_all - right_hi.astype(F32)).astype(BF16)
    for k in range(2):
        total = jnp.zeros((160, 128), F32)
        for m in range(2):
            piece = tile[k, m]
            rows = slice(m * 256, m * 256 + 256)
            total += jnp.dot(piece, right_hi[rows], preferred_element_type=F32)
            total += jnp.dot(piece, right_lo[rows], preferred_element_type=F32)
        part[0, k * 80:k * 80 + 80, 0:128] = total[0:80]
        part[0, k * 80:k * 80 + 80, 128:256] = total[80:160]
    right_part = jnp.concatenate(
        [part[0, 0:80, 0:128], part[0, 0:80, 128:256], part[0, 80:160, 0:128], part[0, 80:160, 128:256]], axis=0
    )
    finished = jnp.dot(left_ref[...], right_part, precision=HIGHEST, preferred_element_type=F32)
    fin[...] = finished.reshape(320, 1, 128)

    def back(i, _):
        to = lax.rem(dp + i, 64)
        pltpu.make_async_remote_copy(
            src_ref=fin.at[pl.ds(to * 5, 5)], dst_ref=ret.at[pl.ds(dp * 5, 5)],
            send_sem=t_s.at[to], recv_sem=t_r.at[dp], device_id=(to, tn), device_id_type=MESH,
        ).start()
        return 0

    lax.fori_loop(1, 64, back, 0)
    ret[pl.ds(dp * 5, 5)] = fin[pl.ds(dp * 5, 5)]

    def back_wait(i, _):
        to = lax.rem(dp + i, 64)
        copy = pltpu.make_async_remote_copy(
            src_ref=fin.at[pl.ds(to * 5, 5)], dst_ref=ret.at[pl.ds(to * 5, 5)],
            send_sem=t_s.at[to], recv_sem=t_r.at[to], device_id=(to, tn), device_id_type=MESH,
        )
        copy.wait_recv()
        copy.wait_send()
        return 0

    lax.fori_loop(1, 64, back_wait, 0)
    for a in range(8):
        for b in range(2):
            first = owner_ref[0, a * 2 + b] * 20
            for w in range(4):
                col = b * 512 + w * 128
                pre_ref[a, :, col:col + 128] = ret[pl.ds(first + w * 5, 5)].reshape(5, 128)

    for copy in sends:
        copy.wait_send()

    @pl.when(jnp.logical_not(stays))
    def _():
        pltpu.make_async_remote_copy(
            src_ref=mine, dst_ref=tile.at[h, c], send_sem=d_s.at[1], recv_sem=d_r.at[h],
            device_id=across, device_id_type=MESH,
        ).wait_send()


def selection():
    sel = np.zeros((256, 160), np.float32)
    for g in range(32):
        for i in range(5):
            sel[8 * g + i, 5 * g + i] = 1.0
    return sel


def shards(inputs, gate_values, up_values, hidden_cotangent, owners, left_inverse, right_inverse):
    xt = inputs.T.reshape(2, 160, 256)
    owner_row = owners[0]
    tiles = jnp.arange(16, dtype=jnp.int32)
    slots = (tiles % 2) * 8 + tiles // 2
    held = jnp.sum(jnp.where(owner_row[None, :] == slots[:, None], tiles[None, :], 0), axis=1)
    pick = jnp.stack([held // 4, (held // 2) % 2, held % 2])
    vmem = pl.BlockSpec(memory_space=pltpu.VMEM)
    smem = pl.BlockSpec(memory_space=pltpu.SMEM)
    scratch = [
        pltpu.VMEM((2, 4, 4, 160, 256), BF16),
        pltpu.VMEM((2, 2, 2, 160, 256), BF16),
        pltpu.VMEM((2, 2, 4, 256, 256), BF16),
        pltpu.VMEM((512, 512), F32),
        pltpu.VMEM((256, 512), F32),
        pltpu.VMEM((4, 160, 256), F32),
        pltpu.VMEM((3, 2, 160, 256), BF16),
        pltpu.VMEM((320, 1, 128), F32),
        pltpu.VMEM((320, 1, 128), F32),
    ]
    for rows in STREAM_ROWS:
        for _ in range(2):
            scratch.append(pltpu.VMEM((2, NARROW, rows, 256), BF16))
            scratch.append(pltpu.VMEM((2, HOPS - NARROW, rows, 256), F32))
    dma = pltpu.SemaphoreType.DMA
    for shape in ((4,), (4,), (4,), (4,), (5,), (5,), (4,), (4,), (8,), (8,), (3, 2, HOPS), (3, 2, HOPS),
                  (2,), (2,), (2,), (2,), (64,), (64,)):
        scratch.append(dma(shape))
    input_rows, output_rows, pre = pl.pallas_call(
        kernel,
        out_shape=(
            jax.ShapeDtypeStruct((5, 320), F32),
            jax.ShapeDtypeStruct((16, 512), F32),
            jax.ShapeDtypeStruct((8, 5, 1024), F32),
        ),
        in_specs=[vmem] * 7 + [smem] * 2,
        out_specs=(vmem, vmem, vmem),
        scratch_shapes=scratch,
        compiler_params=pltpu.CompilerParams(
            collective_id=0, has_side_effects=True, vmem_limit_bytes=48 * 2**20
        ),
        name="kfac",
    )(
        gate_values, up_values, hidden_cotangent, xt, jnp.asarray(selection(), BF16),
        left_inverse[0, 0], right_inverse[0, 0], pick, owners,
    )
    return input_rows[None], output_rows[None], pre


def solution(mesh):
    in_specs = (
        P("dp", "tensor"), P("dp", "tensor"), P("dp", "tensor"), P("dp", "tensor"), P("tensor", None),
        P("dp", "tensor", None, None), P("dp", "tensor", None, None),
    )
    out_specs = (P("tensor", "dp", None), P("tensor", "dp", None), P(None, "dp", "tensor"))
    return jax.shard_map(shards, mesh=mesh, in_specs=in_specs, out_specs=out_specs, check_vma=False)
```

```python
import jax
import jax.numpy as jnp
from jax import lax
from jax.experimental import pallas as pl
from jax.experimental.pallas import tpu as pltpu
from jax.sharding import PartitionSpec as P

MESH = pl.DeviceIdType.MESH
F32 = jnp.float32
BF16 = jnp.bfloat16
Z = 16
REACH = 4
ORDER = (8, 7, 3, 6, 2, 5, 1, 4)
TOTAL = 16384
LEAD = 3
STREAM_ROWS = (80, 80, 80)
STREAM_FIRST = (0, 0, 80)
STREAM_LANES = (128, 256, 256)
LONG_WAY = (0, 0, 1)
TILE_STREAMS = tuple(range(1, len(STREAM_ROWS)))


def split(value):
    high = value.astype(BF16)
    return high, (value - high.astype(F32)).astype(BF16)


def dot3(a, b):
    (a_hi, a_lo), (b_hi, b_lo) = a, b
    total = jnp.dot(a_hi, b_hi, preferred_element_type=F32)
    total += jnp.dot(a_hi, b_lo, preferred_element_type=F32)
    return total + jnp.dot(a_lo, b_hi, preferred_element_type=F32)


def kernel(
    gate_in, up_in, cot_in, xt_in, left_in, right_in, owner_in,
    input_ref, output_ref, pre_ref,
    gates, owner_ref, left_ref, rb, rsplit, lsplit,
    xb, ib, gb, osum, isum, part, piece, rpart, worker_part, fin, ret,
    ring,
    l_s, y_s, y_r, x_s, x_r, cx_s, cx_r, gy_s, gy_r, gc_s, gc_r, r_s, r_r,
    rs_s, rs_r, p_s, p_r, d_s, d_r, t_s, t_r,
):
    dp = lax.axis_index("dp")
    tn = lax.axis_index("tensor")
    h, z, c = dp // 32, (dp // 2) % Z, dp % 2
    x, ylo = tn // 2, tn % 2
    y = h * 2 + ylo
    zbit = z % 2
    home = h == zbit
    away = jnp.logical_not(home)

    def dev(x_, y_, z_, c_):
        return ((y_ // 2) * 32 + z_ * 2 + c_, x_ * 2 + y_ % 2)

    xr, xl, far = (x + 1) % 4, (x + 3) % 4, (x + 2) % 4
    zx = z + 1 - 2 * zbit
    sibling = dev(x, y, z, 1 - c)
    across = dev(x, (y + 2) % 4, z, c)
    right, left = dev(xr, y, z, c), dev(xl, y, z, c)
    step_z = (dev(x, y, (z + 1) % Z, c), dev(x, y, (z + Z - 1) % Z, c))
    leap_z = (dev(x, y, (z + REACH) % Z, c), dev(x, y, (z + Z - REACH) % Z, c))
    pair_z = dev(x, y, zx, c)
    diagonal = dev(x, (y + 2) % 4, zx, c)
    ring_y = [dev(x, (y + k) % 4, z, c) for k in (1, 2, 3)]

    barrier = pltpu.get_barrier_semaphore()
    peers = ring_y + [right, left, sibling, diagonal, *step_z, *leap_z]
    for peer in peers:
        pl.semaphore_signal(barrier, inc=1, device_id=peer, device_id_type=MESH)

    loads = [
        pltpu.make_async_copy(src, dst, l_s.at[k])
        for k, (src, dst) in enumerate((
            (xt_in.at[h], xb.at[c, x, y]), (xt_in, ib.at[c, h]),
            (gate_in, gates.at[0]), (up_in, gates.at[1]), (cot_in, gates.at[2]),
            (owner_in, owner_ref), (left_in, left_ref),
        ))
    ]
    for load in loads:
        load.start()

    def right_slot(which):
        return rb.at[:, pl.ds(pl.multiple_of(which * 128, 128), 128)]

    right_load = pltpu.make_async_copy(right_in, right_slot(zbit), l_s.at[7])
    pl.when(home)(right_load.start)
    pl.semaphore_wait(barrier, len(peers))

    sends = []

    def remote(src, dst, s_sem, r_sem, to):
        return pltpu.make_async_remote_copy(
            src_ref=src, dst_ref=dst, send_sem=s_sem, recv_sem=r_sem, device_id=to, device_id_type=MESH
        )

    def send(src, dst, s_sem, r_sem, to):
        copy = remote(src, dst, s_sem, r_sem, to)
        copy.start()
        sends.append(copy)

    def arrive(dst, s_sem, r_sem):
        remote(dst, dst, s_sem, r_sem, sibling).wait_recv()

    for k in (1, 3):
        half = ((y + k) % 4) // 2
        send(xt_in.at[half], xb.at[c, x, y], y_s.at[k], y_r.at[k], ring_y[k - 1])
    send(xt_in, ib.at[c, h], y_s.at[2], y_r.at[2], across)
    right_away = remote(right_in, right_slot(zbit), r_s.at[0], r_r.at[0], pair_z)
    pl.when(away)(right_away.start)

    def quarter(p, block):
        return 2 * block + p % 2

    for load in loads[2:5]:
        load.wait()
    for p in range(4):
        n = quarter(p, 1 - h if p < 2 else h)
        cols = pl.ds(pl.multiple_of(n * 256, 256), 256)
        pre = gates[0, :, cols].astype(F32)
        s = jax.nn.sigmoid(pre)
        slope = s * (1.0 + pre * (1.0 - s))
        gb[c, h, n] = (gates[2, :, cols].astype(F32) * gates[1, :, cols].astype(F32) * slope).astype(BF16)
        mine = gb.at[c, h, n]
        send(mine, mine, gy_s.at[p], gy_r.at[p], across)
        send(mine, mine, gc_s.at[p], gc_r.at[p], sibling)
    loads[0].wait()
    loads[1].wait()

    for k in (1, 3):
        arrive(xb.at[c, x, (y + 4 - k) % 4], y_s.at[k], y_r.at[k])
    arrive(ib.at[c, 1 - h], y_s.at[2], y_r.at[2])
    xb[c, x, (y + 2) % 4] = ib[c, 1 - h, h]

    def pieces(core, place, k):
        return xb.at[core, place, pl.ds(2 * k, 2)]

    own = (pieces(c, x, 0), pieces(c, x, 1))
    send(own[0], own[0], x_s.at[0], x_r.at[0], right)
    send(own[1], own[1], x_s.at[1], x_r.at[1], left)
    send(own[1], own[1], x_s.at[2], x_r.at[2], right)
    send(own[0], own[0], x_s.at[3], x_r.at[3], left)
    send(xb.at[c, x], xb.at[c, x], cx_s.at[0], cx_r.at[0], sibling)
    send(ib.at[c], ib.at[c], cx_s.at[4], cx_r.at[4], sibling)

    low, high = pieces(c, xl, 0), pieces(c, xr, 1)
    arrive(low, x_s.at[0], x_r.at[0])
    send(low, low, x_s.at[4], x_r.at[4], right)
    arrive(high, x_s.at[1], x_r.at[1])
    send(high, high, x_s.at[5], x_r.at[5], left)

    def pass_gate(p):
        n = quarter(p, h if p < 2 else 1 - h)
        other = gb.at[c, 1 - h, n]
        arrive(other, gy_s.at[p], gy_r.at[p])
        send(other, other, gc_s.at[4 + p], gc_r.at[4 + p], sibling)

    def gate_passed(p):
        arrive(gb.at[1 - c, h, quarter(p, 1 - h if p < 2 else h)], gc_s.at[p], gc_r.at[p])
        arrive(gb.at[1 - c, 1 - h, quarter(p, h if p < 2 else 1 - h)], gc_s.at[4 + p], gc_r.at[4 + p])

    pass_gate(0)
    pass_gate(1)
    arrive(ib.at[1 - c], cx_s.at[4], cx_r.at[4])

    row = lax.broadcasted_iota(jnp.int32, (256, 160), 0)
    col = lax.broadcasted_iota(jnp.int32, (256, 160), 1)
    start = (row >> 4) * 10 + c * 5
    parts = []
    for b in range(3):
        at = (row & 15) - 5 * b
        parts.append(((col == start + at) & (at >= 0) & (at < 5)).astype(F32).astype(BF16))
    total = jnp.zeros((256, 128), F32)
    for k in range(2):
        for m in range(2):
            features = ib[k, m].reshape(320, 256)
            for b in range(3):
                rows = jnp.dot(parts[b], ib[k, m, h], preferred_element_type=F32).astype(BF16)
                columns = features[b * 128:min(b * 128 + 128, 320)]
                term = lax.dot_general(rows, columns, (((1,), (1,)), ((), ())), preferred_element_type=F32)
                if b == 2:
                    term = jnp.concatenate([term, jnp.zeros((256, 64), F32)], axis=1)
                total += term
    isum[...] = total

    for k in range(2):
        arrive(gb.at[1 - c, h, quarter(k, h)], gc_s.at[2 + k], gc_r.at[2 + k])
        arrive(gb.at[1 - c, 1 - h, quarter(k, h)], gc_s.at[4 + k], gc_r.at[4 + k])
    for i in range(2):
        for j in range(2):
            total = jnp.zeros((256, 256), F32)
            for k in range(2):
                for m in range(2):
                    total += lax.dot_general(
                        gb[k, m, 2 * h + i], gb[k, m, 2 * h + j],
                        (((0,), (0,)), ((), ())), preferred_element_type=F32,
                    )
            osum[pl.ds(i * 256, 256), pl.ds(j * 256, 256)] = total

    def held_tile(t):
        slot = (t % 2) * 8 + t // 2
        held = jnp.int32(0)
        for k in range(16):
            held = jnp.maximum(held, jnp.where(owner_ref[0, k] == slot, k, 0))
        return held

    def partial_tile(t, slot):
        held = held_tile(t)
        px, py, pc = held >> 2, (held >> 1) & 1, held & 1
        total = jnp.zeros((160, 256), F32)
        for k in range(2):
            for m in range(2):
                total += jnp.dot(xb[k, px, 2 * m + py], gb[k, m, 2 * pc + c], preferred_element_type=F32)
        part[slot] = total

    def factor_rows(t):
        o_rows = pl.ds(pl.multiple_of(t * 32 + c * 16, 16), 16)
        i_rows = pl.ds(pl.multiple_of(t * 16, 16), 16)
        return jnp.concatenate(
            [osum[o_rows, k * 128:k * 128 + 128] for k in range(4)] + [isum[i_rows, :]], axis=0
        )


    def target(way, distance):
        return (z + distance) % Z if way == 0 else (z + Z - distance) % Z

    def place(index, way):
        return 0 if index == 0 else (index % 2) * 2 + way

    def own_part(stream, index, way):
        if stream == 0:
            return factor_rows(target(way, ORDER[index] if index < 8 else 0))
        return part[place(index, way), pl.ds(STREAM_FIRST[stream], STREAM_ROWS[stream])]

    def landed(stream, way, distance):
        came = ring[stream][0].at[way, distance - 1]
        arrive(came, rs_s.at[stream, way, distance - 1], rs_r.at[stream, way, distance - 1])
        return came[...].astype(F32)

    def hop(stream, index):
        distance = ORDER[index]
        for way in range(2):
            farthest = 8 if way == LONG_WAY[stream] else 7
            if distance > farthest:
                continue
            value = own_part(stream, index, way)
            if distance not in (farthest, REACH - 1):
                value = value + landed(stream, way, distance + 1)
            out = ring[stream][1].at[way, distance - 1]
            out[...] = value.astype(BF16)
            to = leap_z if distance == REACH else step_z
            send(out, ring[stream][0].at[way, distance - 1], rs_s.at[stream, way, distance - 1],
                 rs_r.at[stream, way, distance - 1], to[way])

    def finish(stream):
        value = own_part(stream, 8, 0)
        for distance in (1, REACH):
            for way in range(2):
                value = value + landed(stream, way, distance)
        return value * (1.0 / TOTAL)

    hop(0, 0)
    arrive(pieces(c, xl, 1), x_s.at[2], x_r.at[2])
    send(xb.at[c, xl], xb.at[c, xl], cx_s.at[1], cx_r.at[1], sibling)
    arrive(pieces(c, xr, 0), x_s.at[3], x_r.at[3])
    send(xb.at[c, xr], xb.at[c, xr], cx_s.at[2], cx_r.at[2], sibling)
    hop(0, 1)
    pass_gate(2)
    pass_gate(3)
    hop(0, 2)
    arrive(pieces(c, far, 0), x_s.at[4], x_r.at[4])
    arrive(pieces(c, far, 1), x_s.at[5], x_r.at[5])
    send(xb.at[c, far], xb.at[c, far], cx_s.at[3], cx_r.at[3], sibling)
    loads[5].wait()
    for k in range(2):
        arrive(gb.at[1 - c, h, quarter(k, 1 - h)], gc_s.at[k], gc_r.at[k])
        arrive(gb.at[1 - c, 1 - h, quarter(k, 1 - h)], gc_s.at[6 + k], gc_r.at[6 + k])
    for k, at in enumerate((x, xl, xr, far)):
        arrive(xb.at[1 - c, at], cx_s.at[k], cx_r.at[k])

    right_on = remote(rb, rb, r_s.at[1], r_r.at[1], across)

    for step in range(8):
        if step == 0:
            partial_tile(target(0, ORDER[0]), 0)
        ahead = [(step + 1, way) for way in range(2 if step < 7 else 1)]
        for k, stream in enumerate(TILE_STREAMS):
            hop(stream, step)
            if k % (len(TILE_STREAMS) // 2) == 0 and ahead:
                to, way = ahead.pop(0)
                partial_tile(target(way, ORDER[to] if to < 8 else 0), place(to, way))
        if step + LEAD < 8:
            hop(0, step + LEAD)
        if step == 0:
            @pl.when(home)
            def _():
                right_load.wait()
                arrive(right_slot(1 - zbit), r_s.at[0], r_r.at[0])
                right_on.start()
            loads[6].wait()
            lsplit[0], lsplit[1] = split(left_ref[...])
        if step == 5:
            pl.when(away)(right_on.wait_recv)
            rsplit[0], rsplit[1] = split(rb[...])
            factors = finish(0)
            for k in range(4):
                output_ref[:, k * 128:k * 128 + 128] = factors[k * 16:k * 16 + 16]
            input_ref[:, 0:128] = factors[64:69]
            input_ref[:, 128:256] = factors[69:74]
            input_ref[:, 256:320] = factors[74:79, 0:64]

    for i in range(2):
        for stream in TILE_STREAMS:
            first = STREAM_FIRST[stream] - i * 80
            if 0 <= first < 80:
                piece[c, i, pl.ds(first, STREAM_ROWS[stream])] = finish(stream)
        mine = piece.at[c, i]
        send(mine, mine, p_s.at[i], p_r.at[i], sibling)
    goes = dev(x, zbit * 2 + ylo, zx, c)
    stay_copies = []
    for i in range(2):
        arrive(piece.at[1 - c, i], p_s.at[i], p_r.at[i])
        total = jnp.zeros((80, 256), F32)
        for k in range(2):
            rows = slice(k * 256, k * 256 + 256)
            total += dot3(split(piece[k, i]), (rsplit[0, rows], rsplit[1, rows]))
        rpart[0, i] = total[:, 0:128]
        rpart[1, i] = total[:, 128:256]
        send(rpart.at[1 - zbit, i], worker_part.at[h, i], d_s.at[i], d_r.at[h, i], goes)
        stay_copies.append(remote(rpart.at[zbit, i], worker_part.at[h, i], d_s.at[2 + i], d_r.at[h, i], across))
        pl.when(away)(stay_copies[i].start)

    @pl.when(home)
    def _():
        worker_part[h] = rpart[zbit]

    for i in range(2):
        @pl.when(away)
        def _():
            arrive(worker_part.at[h, i], d_s.at[i], d_r.at[h, i])
        arrive(worker_part.at[1 - h, i], d_s.at[i], d_r.at[1 - h, i])
    right_part = worker_part[...].reshape(320, 128)
    finished = dot3((lsplit[0], lsplit[1]), split(right_part))
    fin[...] = finished.reshape(320, 1, 128)

    def back_copy(to, at):
        return remote(fin.at[pl.ds(to * 5, 5)], ret.at[pl.ds(at * 5, 5)], t_s.at[to], t_r.at[at], (to, tn))

    def back(i, _):
        back_copy(lax.rem(dp + i, 64), dp).start()
        return 0

    lax.fori_loop(1, 64, back, 0)
    ret[pl.ds(dp * 5, 5)] = fin[pl.ds(dp * 5, 5)]

    def back_wait(i, _):
        to = lax.rem(dp + i, 64)
        copy = back_copy(to, to)
        copy.wait_recv()
        copy.wait_send()
        return 0

    lax.fori_loop(1, 64, back_wait, 0)
    for a in range(8):
        for b in range(2):
            first = jnp.clip(owner_ref[0, a * 2 + b], 0, 15) * 20
            for w in range(4):
                at = b * 512 + w * 128
                pre_ref[:, a:a + 1, at:at + 128] = ret[pl.ds(first + w * 5, 5)]

    for copy in sends:
        copy.wait_send()

    @pl.when(home)
    def _():
        right_on.wait_send()

    @pl.when(away)
    def _():
        right_away.wait_send()
        for copy in stay_copies:
            copy.wait_send()


def shards(inputs, gate_values, up_values, hidden_cotangent, owners, left_inverse, right_inverse):
    xt = inputs.T.reshape(2, 160, 256)
    vmem = pl.BlockSpec(memory_space=pltpu.VMEM)
    hbm = pl.BlockSpec(memory_space=pltpu.HBM)
    scratch = [
        pltpu.VMEM((3, 256, 1024), BF16),
        pltpu.SMEM((1, 16), jnp.int32),
        pltpu.VMEM((320, 320), F32),
        pltpu.VMEM((512, 256), F32),
        pltpu.VMEM((2, 512, 256), BF16),
        pltpu.VMEM((2, 320, 320), BF16),
        pltpu.VMEM((2, 4, 4, 160, 256), BF16),
        pltpu.VMEM((2, 2, 2, 160, 256), BF16),
        pltpu.VMEM((2, 2, 4, 256, 256), BF16),
        pltpu.VMEM((512, 512), F32),
        pltpu.VMEM((256, 128), F32),
        pltpu.VMEM((4, 160, 256), F32),
        pltpu.VMEM((2, 2, 80, 256), F32),
        pltpu.VMEM((2, 2, 80, 128), F32),
        pltpu.VMEM((2, 2, 80, 128), F32),
        pltpu.VMEM((320, 1, 128), F32),
        pltpu.VMEM((320, 1, 128), F32),
    ]
    scratch.append([
        [pltpu.VMEM((2, 8, rows, lanes), BF16)] * 2
        for rows, lanes in zip(STREAM_ROWS, STREAM_LANES)
    ])
    dma = pltpu.SemaphoreType.DMA
    for shape in ((8,), (4,), (4,), (6,), (6,), (5,), (5,), (4,), (4,), (8,), (8,), (2,), (2,),
                  (len(STREAM_ROWS), 2, 8), (len(STREAM_ROWS), 2, 8), (2,), (2,), (4,), (2, 2), (64,), (64,)):
        scratch.append(dma(shape))
    input_rows, output_rows, pre = pl.pallas_call(
        kernel,
        out_shape=(
            jax.ShapeDtypeStruct((5, 320), F32),
            jax.ShapeDtypeStruct((16, 512), F32),
            jax.ShapeDtypeStruct((5, 8, 1024), F32),
        ),
        in_specs=[hbm] * 7,
        out_specs=(vmem, vmem, vmem),
        scratch_shapes=scratch,
        compiler_params=pltpu.CompilerParams(
            collective_id=0, has_side_effects=True, vmem_limit_bytes=62 * 2**20
        ),
        name="kfac",
    )(
        gate_values, up_values, hidden_cotangent, xt, left_inverse[0, 0], right_inverse[0, 0], owners,
    )
    return input_rows[None], output_rows[None], pre.transpose(1, 0, 2)


def solution(mesh):
    in_specs = (
        P("dp", "tensor"), P("dp", "tensor"), P("dp", "tensor"), P("dp", "tensor"), P("tensor", None),
        P("dp", "tensor", None, None), P("dp", "tensor", None, None),
    )
    out_specs = (P("tensor", "dp", None), P("tensor", "dp", None), P(None, "dp", "tensor"))
    return jax.shard_map(shards, mesh=mesh, in_specs=in_specs, out_specs=out_specs, check_vma=False)
```

```python
import jax
import jax.numpy as jnp
from jax import lax
from jax.experimental import pallas as pl
from jax.experimental.pallas import tpu as pltpu
from jax.sharding import PartitionSpec as P

MESH = pl.DeviceIdType.MESH
F32 = jnp.float32
BF16 = jnp.bfloat16
Z = 16
REACH = 4
ORDER = (8, 7, 3, 6, 2, 5, 1, 4)
TOTAL = 16384
LEAD = 3
STREAM_ROWS = (80, 80, 80)
STREAM_FIRST = (0, 0, 80)
STREAM_LANES = (128, 256, 256)
LONG_WAY = (0, 0, 1)
TILE_STREAMS = tuple(range(1, len(STREAM_ROWS)))


def split(value):
    high = value.astype(BF16)
    return high, (value - high.astype(F32)).astype(BF16)


def dot3(a, b):
    (a_hi, a_lo), (b_hi, b_lo) = a, b
    total = jnp.dot(a_hi, b_hi, preferred_element_type=F32)
    total += jnp.dot(a_hi, b_lo, preferred_element_type=F32)
    return total + jnp.dot(a_lo, b_hi, preferred_element_type=F32)


def kernel(
    gate_in, up_in, cot_in, xt_in, left_in, right_in, owner_in,
    input_ref, output_ref, pre_ref,
    gates, owner_ref, left_ref, rb, rsplit, lsplit,
    xb, ib, gb, relay, osum, isum, part, piece, rpart, worker_part, fin, ret,
    ring,
    l_s, y_s, y_r, x_s, x_r, cx_s, cx_r, gr_s, gr_r, gy_s, gy_r, gc_s, gc_r, r_s, r_r,
    rs_s, rs_r, p_s, p_r, d_s, d_r, t_s, t_r,
):
    dp = lax.axis_index("dp")
    tn = lax.axis_index("tensor")
    h, z, c = dp // 32, (dp // 2) % Z, dp % 2
    x, ylo = tn // 2, tn % 2
    y = h * 2 + ylo
    zbit = z % 2
    home = h == zbit
    away = jnp.logical_not(home)

    def dev(x_, y_, z_, c_):
        return ((y_ // 2) * 32 + z_ * 2 + c_, x_ * 2 + y_ % 2)

    xr, xl, far = (x + 1) % 4, (x + 3) % 4, (x + 2) % 4
    zx = z + 1 - 2 * zbit
    sibling = dev(x, y, z, 1 - c)
    across = dev(x, (y + 2) % 4, z, c)
    right, left = dev(xr, y, z, c), dev(xl, y, z, c)
    step_z = (dev(x, y, (z + 1) % Z, c), dev(x, y, (z + Z - 1) % Z, c))
    leap_z = (dev(x, y, (z + REACH) % Z, c), dev(x, y, (z + Z - REACH) % Z, c))
    pair_z = dev(x, y, zx, c)
    diagonal = dev(x, (y + 2) % 4, zx, c)
    ring_y = [dev(x, (y + k) % 4, z, c) for k in (1, 2, 3)]

    barrier = pltpu.get_barrier_semaphore()
    peers = ring_y + [right, left, sibling, diagonal, *step_z, *leap_z]
    for peer in peers:
        pl.semaphore_signal(barrier, inc=1, device_id=peer, device_id_type=MESH)

    loads = [
        pltpu.make_async_copy(src, dst, l_s.at[k])
        for k, (src, dst) in enumerate((
            (xt_in.at[h], xb.at[c, x, y]), (xt_in, ib.at[c, h]),
            (gate_in, gates.at[0]), (up_in, gates.at[1]), (cot_in, gates.at[2]),
            (owner_in, owner_ref), (left_in, left_ref),
        ))
    ]
    for load in loads:
        load.start()

    def right_slot(which):
        return rb.at[:, pl.ds(pl.multiple_of(which * 128, 128), 128)]

    right_load = pltpu.make_async_copy(right_in, right_slot(zbit), l_s.at[7])
    pl.when(home)(right_load.start)
    pl.semaphore_wait(barrier, len(peers))

    sends = []

    def remote(src, dst, s_sem, r_sem, to):
        return pltpu.make_async_remote_copy(
            src_ref=src, dst_ref=dst, send_sem=s_sem, recv_sem=r_sem, device_id=to, device_id_type=MESH
        )

    def send(src, dst, s_sem, r_sem, to):
        copy = remote(src, dst, s_sem, r_sem, to)
        copy.start()
        sends.append(copy)

    def arrive(dst, s_sem, r_sem):
        remote(dst, dst, s_sem, r_sem, sibling).wait_recv()

    for k in (1, 3, 2):
        half = ((y + k) % 4) // 2
        send(xt_in.at[half], xb.at[c, x, y], y_s.at[k], y_r.at[k], ring_y[k - 1])
    right_away = remote(right_in, right_slot(zbit), r_s.at[0], r_r.at[0], pair_z)
    pl.when(away)(right_away.start)

    def quarter(p, block):
        return 2 * block + p % 2

    for load in loads[2:5]:
        load.wait()
    for p in range(4):
        n = quarter(p, 1 - h if p < 2 else h)
        cols = pl.ds(pl.multiple_of(n * 256, 256), 256)
        pre = gates[0, :, cols].astype(F32)
        s = jax.nn.sigmoid(pre)
        slope = s * (1.0 + pre * (1.0 - s))
        gb[c, h, n] = (gates[2, :, cols].astype(F32) * gates[1, :, cols].astype(F32) * slope).astype(BF16)
        mine = gb.at[c, h, n]
        send(mine, relay.at[p], gr_s.at[p], gr_r.at[p], ring_y[2 * (p % 2)])
        send(mine, mine, gc_s.at[p], gc_r.at[p], sibling)
        if p == 1:
            send(xt_in.at[h], ib.at[c, h, h], y_s.at[0], y_r.at[0], across)
    loads[0].wait()
    loads[1].wait()

    for k in (1, 3, 2):
        arrive(xb.at[c, x, (y + 4 - k) % 4], y_s.at[k], y_r.at[k])

    def pieces(core, place, k):
        return xb.at[core, place, pl.ds(2 * k, 2)]

    own = (pieces(c, x, 0), pieces(c, x, 1))
    send(own[0], own[0], x_s.at[0], x_r.at[0], right)
    send(own[1], own[1], x_s.at[1], x_r.at[1], left)
    send(own[1], own[1], x_s.at[2], x_r.at[2], right)
    send(own[0], own[0], x_s.at[3], x_r.at[3], left)
    send(xb.at[c, x], xb.at[c, x], cx_s.at[0], cx_r.at[0], sibling)
    ib[c, 1 - h, h] = xb[c, x, (y + 2) % 4]

    def pass_relay(p):
        here = relay.at[p]
        arrive(here, gr_s.at[p], gr_r.at[p])
        half = ((y + (3 if p % 2 == 0 else 1)) % 4) // 2
        n = quarter(p, 1 - half if p < 2 else half)
        send(here, gb.at[c, half, n], gy_s.at[p], gy_r.at[p], ring_y[2 * (p % 2)])

    pass_relay(0)
    pass_relay(1)

    low, high = pieces(c, xl, 0), pieces(c, xr, 1)
    arrive(low, x_s.at[0], x_r.at[0])
    send(low, low, x_s.at[4], x_r.at[4], right)
    arrive(high, x_s.at[1], x_r.at[1])
    send(high, high, x_s.at[5], x_r.at[5], left)
    pass_relay(2)
    pass_relay(3)

    def pass_gate(p):
        n = quarter(p, h if p < 2 else 1 - h)
        other = gb.at[c, 1 - h, n]
        arrive(other, gy_s.at[p], gy_r.at[p])
        send(other, other, gc_s.at[4 + p], gc_r.at[4 + p], sibling)

    def gate_passed(p):
        arrive(gb.at[1 - c, h, quarter(p, 1 - h if p < 2 else h)], gc_s.at[p], gc_r.at[p])
        arrive(gb.at[1 - c, 1 - h, quarter(p, h if p < 2 else 1 - h)], gc_s.at[4 + p], gc_r.at[4 + p])

    pass_gate(0)
    pass_gate(1)
    arrive(ib.at[c, 1 - h, 1 - h], y_s.at[0], y_r.at[0])
    send(ib.at[c], ib.at[c], cx_s.at[4], cx_r.at[4], sibling)
    arrive(ib.at[1 - c], cx_s.at[4], cx_r.at[4])

    row = lax.broadcasted_iota(jnp.int32, (256, 160), 0)
    col = lax.broadcasted_iota(jnp.int32, (256, 160), 1)
    start = (row >> 4) * 10 + c * 5
    parts = []
    for b in range(3):
        at = (row & 15) - 5 * b
        parts.append(((col == start + at) & (at >= 0) & (at < 5)).astype(F32).astype(BF16))
    total = jnp.zeros((256, 128), F32)
    for k in range(2):
        for m in range(2):
            features = ib[k, m].reshape(320, 256)
            for b in range(3):
                rows = jnp.dot(parts[b], ib[k, m, h], preferred_element_type=F32).astype(BF16)
                columns = features[b * 128:min(b * 128 + 128, 320)]
                term = lax.dot_general(rows, columns, (((1,), (1,)), ((), ())), preferred_element_type=F32)
                if b == 2:
                    term = jnp.concatenate([term, jnp.zeros((256, 64), F32)], axis=1)
                total += term
    isum[...] = total

    for k in range(2):
        arrive(gb.at[1 - c, h, quarter(k, h)], gc_s.at[2 + k], gc_r.at[2 + k])
        arrive(gb.at[1 - c, 1 - h, quarter(k, h)], gc_s.at[4 + k], gc_r.at[4 + k])
    for i in range(2):
        for j in range(2):
            total = jnp.zeros((256, 256), F32)
            for k in range(2):
                for m in range(2):
                    total += lax.dot_general(
                        gb[k, m, 2 * h + i], gb[k, m, 2 * h + j],
                        (((0,), (0,)), ((), ())), preferred_element_type=F32,
                    )
            osum[pl.ds(i * 256, 256), pl.ds(j * 256, 256)] = total

    def held_tile(t):
        slot = (t % 2) * 8 + t // 2
        held = jnp.int32(0)
        for k in range(16):
            held = jnp.maximum(held, jnp.where(owner_ref[0, k] == slot, k, 0))
        return held

    def partial_tile(t, slot):
        held = held_tile(t)
        px, py, pc = held >> 2, (held >> 1) & 1, held & 1
        total = jnp.zeros((160, 256), F32)
        for k in range(2):
            for m in range(2):
                total += jnp.dot(xb[k, px, 2 * m + py], gb[k, m, 2 * pc + c], preferred_element_type=F32)
        part[slot] = total

    def factor_rows(t):
        o_rows = pl.ds(pl.multiple_of(t * 32 + c * 16, 16), 16)
        i_rows = pl.ds(pl.multiple_of(t * 16, 16), 16)
        return jnp.concatenate(
            [osum[o_rows, k * 128:k * 128 + 128] for k in range(4)] + [isum[i_rows, :]], axis=0
        )


    def target(way, distance):
        return (z + distance) % Z if way == 0 else (z + Z - distance) % Z

    def place(index, way):
        return 0 if index == 0 else (index % 2) * 2 + way

    def own_part(stream, index, way):
        if stream == 0:
            return factor_rows(target(way, ORDER[index] if index < 8 else 0))
        return part[place(index, way), pl.ds(STREAM_FIRST[stream], STREAM_ROWS[stream])]

    def landed(stream, way, distance):
        came = ring[stream][0].at[way, distance - 1]
        arrive(came, rs_s.at[stream, way, distance - 1], rs_r.at[stream, way, distance - 1])
        return came[...].astype(F32)

    def hop(stream, index):
        distance = ORDER[index]
        for way in range(2):
            farthest = 8 if way == LONG_WAY[stream] else 7
            if distance > farthest:
                continue
            value = own_part(stream, index, way)
            if distance not in (farthest, REACH - 1):
                value = value + landed(stream, way, distance + 1)
            out = ring[stream][1].at[way, distance - 1]
            out[...] = value.astype(BF16)
            to = leap_z if distance == REACH else step_z
            send(out, ring[stream][0].at[way, distance - 1], rs_s.at[stream, way, distance - 1],
                 rs_r.at[stream, way, distance - 1], to[way])

    def finish(stream):
        value = own_part(stream, 8, 0)
        for distance in (1, REACH):
            for way in range(2):
                value = value + landed(stream, way, distance)
        return value * (1.0 / TOTAL)

    hop(0, 0)
    arrive(pieces(c, xl, 1), x_s.at[2], x_r.at[2])
    send(xb.at[c, xl], xb.at[c, xl], cx_s.at[1], cx_r.at[1], sibling)
    arrive(pieces(c, xr, 0), x_s.at[3], x_r.at[3])
    send(xb.at[c, xr], xb.at[c, xr], cx_s.at[2], cx_r.at[2], sibling)
    hop(0, 1)
    pass_gate(2)
    pass_gate(3)
    hop(0, 2)
    arrive(pieces(c, far, 0), x_s.at[4], x_r.at[4])
    arrive(pieces(c, far, 1), x_s.at[5], x_r.at[5])
    send(xb.at[c, far], xb.at[c, far], cx_s.at[3], cx_r.at[3], sibling)
    loads[5].wait()
    for k in range(2):
        arrive(gb.at[1 - c, h, quarter(k, 1 - h)], gc_s.at[k], gc_r.at[k])
        arrive(gb.at[1 - c, 1 - h, quarter(k, 1 - h)], gc_s.at[6 + k], gc_r.at[6 + k])
    for k, at in enumerate((x, xl, xr, far)):
        arrive(xb.at[1 - c, at], cx_s.at[k], cx_r.at[k])

    right_on = remote(rb, rb, r_s.at[1], r_r.at[1], across)

    for step in range(8):
        if step == 0:
            partial_tile(target(0, ORDER[0]), 0)
        ahead = [(step + 1, way) for way in range(2 if step < 7 else 1)]
        for k, stream in enumerate(TILE_STREAMS):
            hop(stream, step)
            if k % (len(TILE_STREAMS) // 2) == 0 and ahead:
                to, way = ahead.pop(0)
                partial_tile(target(way, ORDER[to] if to < 8 else 0), place(to, way))
        if step + LEAD < 8:
            hop(0, step + LEAD)
        if step == 0:
            @pl.when(home)
            def _():
                right_load.wait()
                arrive(right_slot(1 - zbit), r_s.at[0], r_r.at[0])
                right_on.start()
            loads[6].wait()
            lsplit[0], lsplit[1] = split(left_ref[...])
        if step == 5:
            pl.when(away)(right_on.wait_recv)
            rsplit[0], rsplit[1] = split(rb[...])
            factors = finish(0)
            for k in range(4):
                output_ref[:, k * 128:k * 128 + 128] = factors[k * 16:k * 16 + 16]
            for r in range(5):
                input_ref[r, :, 0:128] = factors[64 + r:65 + r]
                input_ref[r, :, 128:256] = factors[69 + r:70 + r]
                input_ref[r, :, 256:320] = factors[74 + r:75 + r, 0:64]

    for i in range(2):
        for stream in TILE_STREAMS:
            first = STREAM_FIRST[stream] - i * 80
            if 0 <= first < 80:
                piece[c, i, pl.ds(first, STREAM_ROWS[stream])] = finish(stream)
        mine = piece.at[c, i]
        send(mine, mine, p_s.at[i], p_r.at[i], sibling)
    goes = dev(x, zbit * 2 + ylo, zx, c)
    stay_copies = []
    for i in range(2):
        arrive(piece.at[1 - c, i], p_s.at[i], p_r.at[i])
        total = jnp.zeros((80, 256), F32)
        for k in range(2):
            rows = slice(k * 256, k * 256 + 256)
            total += dot3(split(piece[k, i]), (rsplit[0, rows], rsplit[1, rows]))
        rpart[0, i] = total[:, 0:128]
        rpart[1, i] = total[:, 128:256]
        send(rpart.at[1 - zbit, i], worker_part.at[h, i], d_s.at[i], d_r.at[h, i], goes)
        stay_copies.append(remote(rpart.at[zbit, i], worker_part.at[h, i], d_s.at[2 + i], d_r.at[h, i], across))
        pl.when(away)(stay_copies[i].start)

    @pl.when(home)
    def _():
        worker_part[h] = rpart[zbit]

    for i in range(2):
        @pl.when(away)
        def _():
            arrive(worker_part.at[h, i], d_s.at[i], d_r.at[h, i])
        arrive(worker_part.at[1 - h, i], d_s.at[i], d_r.at[1 - h, i])
    right_part = worker_part[...].reshape(320, 128)
    finished = dot3((lsplit[0], lsplit[1]), split(right_part))
    fin[...] = finished.reshape(320, 1, 128)

    def back_copy(to, at):
        return remote(fin.at[pl.ds(to * 5, 5)], ret.at[pl.ds(at * 5, 5)], t_s.at[to], t_r.at[at], (to, tn))

    def back(i, _):
        back_copy(lax.rem(dp + i, 64), dp).start()
        return 0

    lax.fori_loop(1, 64, back, 0)
    ret[pl.ds(dp * 5, 5)] = fin[pl.ds(dp * 5, 5)]

    def back_wait(i, _):
        to = lax.rem(dp + i, 64)
        copy = back_copy(to, to)
        copy.wait_recv()
        copy.wait_send()
        return 0

    lax.fori_loop(1, 64, back_wait, 0)
    for a in range(8):
        for b in range(2):
            first = jnp.clip(owner_ref[0, a * 2 + b], 0, 15) * 20
            for w in range(4):
                at = b * 512 + w * 128
                pre_ref[:, a:a + 1, at:at + 128] = ret[pl.ds(first + w * 5, 5)]

    for copy in sends:
        copy.wait_send()

    @pl.when(home)
    def _():
        right_on.wait_send()

    @pl.when(away)
    def _():
        right_away.wait_send()
        for copy in stay_copies:
            copy.wait_send()


def store(a_in, b_in, c_in, a_out, b_out, c_out, sems):
    copies = [
        pltpu.make_async_copy(src, dst, sems.at[k])
        for k, (src, dst) in enumerate(((a_in, a_out), (b_in, b_out), (c_in, c_out)))
    ]
    for copy in copies:
        copy.start()
    for copy in copies:
        copy.wait()


def shards(inputs, gate_values, up_values, hidden_cotangent, owners, left_inverse, right_inverse):
    xt = inputs.T.reshape(2, 160, 256)
    vmem = pl.BlockSpec(memory_space=pltpu.VMEM)
    hbm = pl.BlockSpec(memory_space=pltpu.HBM)
    scratch = [
        pltpu.VMEM((3, 256, 1024), BF16),
        pltpu.SMEM((1, 16), jnp.int32),
        pltpu.VMEM((320, 320), F32),
        pltpu.VMEM((512, 256), F32),
        pltpu.VMEM((2, 512, 256), BF16),
        pltpu.VMEM((2, 320, 320), BF16),
        pltpu.VMEM((2, 4, 4, 160, 256), BF16),
        pltpu.VMEM((2, 2, 2, 160, 256), BF16),
        pltpu.VMEM((2, 2, 4, 256, 256), BF16),
        pltpu.VMEM((4, 256, 256), BF16),
        pltpu.VMEM((512, 512), F32),
        pltpu.VMEM((256, 128), F32),
        pltpu.VMEM((4, 160, 256), F32),
        pltpu.VMEM((2, 2, 80, 256), F32),
        pltpu.VMEM((2, 2, 80, 128), F32),
        pltpu.VMEM((2, 2, 80, 128), F32),
        pltpu.VMEM((320, 1, 128), F32),
        pltpu.VMEM((320, 1, 128), F32),
    ]
    scratch.append([
        [pltpu.VMEM((2, 8, rows, lanes), BF16)] * 2
        for rows, lanes in zip(STREAM_ROWS, STREAM_LANES)
    ])
    dma = pltpu.SemaphoreType.DMA
    for shape in ((8,), (4,), (4,), (6,), (6,), (5,), (5,), (4,), (4,), (4,), (4,), (8,), (8,), (2,), (2,),
                  (len(STREAM_ROWS), 2, 8), (len(STREAM_ROWS), 2, 8), (2,), (2,), (4,), (2, 2), (64,), (64,)):
        scratch.append(dma(shape))
    input_rows, output_rows, pre = pl.pallas_call(
        kernel,
        out_shape=(
            jax.ShapeDtypeStruct((5, 1, 320), F32),
            jax.ShapeDtypeStruct((16, 512), F32),
            jax.ShapeDtypeStruct((5, 8, 1024), F32),
        ),
        in_specs=[hbm] * 7,
        out_specs=(vmem, vmem, vmem),
        scratch_shapes=scratch,
        compiler_params=pltpu.CompilerParams(
            collective_id=0, has_side_effects=True, vmem_limit_bytes=62 * 2**20
        ),
        name="kfac",
    )(
        gate_values, up_values, hidden_cotangent, xt, left_inverse[0, 0], right_inverse[0, 0], owners,
    )
    results = (input_rows, output_rows, pre)
    input_rows, output_rows, pre = pl.pallas_call(
        store,
        out_shape=tuple(jax.ShapeDtypeStruct(r.shape, F32) for r in results),
        in_specs=[hbm] * 3,
        out_specs=(hbm,) * 3,
        scratch_shapes=[dma((3,))],
        compiler_params=pltpu.CompilerParams(vmem_limit_bytes=62 * 2**20),
        name="store",
    )(*results)
    return input_rows.transpose(1, 0, 2), output_rows[None], pre.transpose(1, 0, 2)


def solution(mesh):
    in_specs = (
        P("dp", "tensor"), P("dp", "tensor"), P("dp", "tensor"), P("dp", "tensor"), P("tensor", None),
        P("dp", "tensor", None, None), P("dp", "tensor", None, None),
    )
    out_specs = (P("tensor", "dp", None), P("tensor", "dp", None), P(None, "dp", "tensor"))
    return jax.shard_map(shards, mesh=mesh, in_specs=in_specs, out_specs=out_specs, check_vma=False)
```

```python
import jax
import jax.numpy as jnp
from jax import lax
from jax.experimental import pallas as pl
from jax.experimental.pallas import tpu as pltpu
from jax.sharding import PartitionSpec as P

MESH = pl.DeviceIdType.MESH
F32 = jnp.float32
BF16 = jnp.bfloat16
Z = 16
REACH = 4
ORDER = (8, 7, 3, 6, 2, 5, 1, 4)
TOTAL = 16384
LEAD = 1
STREAM_ROWS = (80, 80, 80)
STREAM_FIRST = (0, 0, 80)
STREAM_LANES = (128, 256, 256)
LONG_WAY = (0, 0, 1)
TILE_STREAMS = tuple(range(1, len(STREAM_ROWS)))


def split(value):
    high = value.astype(BF16)
    return high, (value - high.astype(F32)).astype(BF16)


def dot3(a, b):
    (a_hi, a_lo), (b_hi, b_lo) = a, b
    total = jnp.dot(a_hi, b_hi, preferred_element_type=F32)
    total += jnp.dot(a_hi, b_lo, preferred_element_type=F32)
    return total + jnp.dot(a_lo, b_hi, preferred_element_type=F32)


def kernel(
    gate_in, up_in, cot_in, xt_in, left_in, right_in, owner_in,
    input_ref, output_ref, pre_ref,
    gates, owner_ref, left_ref, rb, rsplit, lsplit,
    xb, ib, gb, relay, osum, isum, part, piece, rpart, worker_part, fin, ret,
    ring,
    l_s, y_s, y_r, x_s, x_r, cx_s, cx_r, gr_s, gr_r, gy_s, gy_r, gc_s, gc_r, r_s, r_r,
    rs_s, rs_r, p_s, p_r, d_s, d_r, t_s, t_r,
):
    dp = lax.axis_index("dp")
    tn = lax.axis_index("tensor")
    h, z, c = dp // 32, (dp // 2) % Z, dp % 2
    x, ylo = tn // 2, tn % 2
    y = h * 2 + ylo
    zbit = z % 2
    home = h == zbit
    away = jnp.logical_not(home)

    def dev(x_, y_, z_, c_):
        return ((y_ // 2) * 32 + z_ * 2 + c_, x_ * 2 + y_ % 2)

    xr, xl, far = (x + 1) % 4, (x + 3) % 4, (x + 2) % 4
    zx = z + 1 - 2 * zbit
    sibling = dev(x, y, z, 1 - c)
    across = dev(x, (y + 2) % 4, z, c)
    right, left = dev(xr, y, z, c), dev(xl, y, z, c)
    step_z = (dev(x, y, (z + 1) % Z, c), dev(x, y, (z + Z - 1) % Z, c))
    leap_z = (dev(x, y, (z + REACH) % Z, c), dev(x, y, (z + Z - REACH) % Z, c))
    pair_z = dev(x, y, zx, c)
    diagonal = dev(x, (y + 2) % 4, zx, c)
    ring_y = [dev(x, (y + k) % 4, z, c) for k in (1, 2, 3)]

    barrier = pltpu.get_barrier_semaphore()
    peers = ring_y + [right, left, sibling, diagonal, *step_z, *leap_z]
    for peer in peers:
        pl.semaphore_signal(barrier, inc=1, device_id=peer, device_id_type=MESH)

    loads = [
        pltpu.make_async_copy(src, dst, l_s.at[k])
        for k, (src, dst) in enumerate((
            (xt_in.at[h], xb.at[c, x, y]), (xt_in, ib.at[c, h]),
            (gate_in, gates.at[0]), (up_in, gates.at[1]), (cot_in, gates.at[2]),
            (owner_in, owner_ref), (left_in, left_ref),
        ))
    ]
    for load in loads:
        load.start()

    def right_slot(which):
        return rb.at[:, pl.ds(pl.multiple_of(which * 128, 128), 128)]

    right_load = pltpu.make_async_copy(right_in, right_slot(zbit), l_s.at[7])
    pl.when(home)(right_load.start)
    pl.semaphore_wait(barrier, len(peers))

    sends = []

    def remote(src, dst, s_sem, r_sem, to):
        return pltpu.make_async_remote_copy(
            src_ref=src, dst_ref=dst, send_sem=s_sem, recv_sem=r_sem, device_id=to, device_id_type=MESH
        )

    def send(src, dst, s_sem, r_sem, to):
        copy = remote(src, dst, s_sem, r_sem, to)
        copy.start()
        sends.append(copy)

    def arrive(dst, s_sem, r_sem):
        remote(dst, dst, s_sem, r_sem, sibling).wait_recv()

    for k in (1, 3, 2):
        half = ((y + k) % 4) // 2
        send(xt_in.at[half], xb.at[c, x, y], y_s.at[k], y_r.at[k], ring_y[k - 1])
    right_away = remote(right_in, right_slot(zbit), r_s.at[0], r_r.at[0], pair_z)
    pl.when(away)(right_away.start)

    def quarter(p, block):
        return 2 * block + p % 2

    for load in loads[2:5]:
        load.wait()
    for p in range(4):
        n = quarter(p, 1 - h if p < 2 else h)
        cols = pl.ds(pl.multiple_of(n * 256, 256), 256)
        pre = gates[0, :, cols].astype(F32)
        s = jax.nn.sigmoid(pre)
        slope = s * (1.0 + pre * (1.0 - s))
        gb[c, h, n] = (gates[2, :, cols].astype(F32) * gates[1, :, cols].astype(F32) * slope).astype(BF16)
        mine = gb.at[c, h, n]
        send(mine, relay.at[p], gr_s.at[p], gr_r.at[p], ring_y[2 * (p % 2)])
        send(mine, mine, gc_s.at[p], gc_r.at[p], sibling)
        if p == 1:
            send(xt_in.at[h], ib.at[c, h, h], y_s.at[0], y_r.at[0], across)
    loads[0].wait()
    loads[1].wait()

    for k in (1, 3, 2):
        arrive(xb.at[c, x, (y + 4 - k) % 4], y_s.at[k], y_r.at[k])

    def pieces(core, place, k):
        return xb.at[core, place, pl.ds(2 * k, 2)]

    own = (pieces(c, x, 0), pieces(c, x, 1))
    send(own[0], own[0], x_s.at[0], x_r.at[0], right)
    send(own[1], own[1], x_s.at[1], x_r.at[1], left)
    send(own[1], own[1], x_s.at[2], x_r.at[2], right)
    send(own[0], own[0], x_s.at[3], x_r.at[3], left)
    send(xb.at[c, x], xb.at[c, x], cx_s.at[0], cx_r.at[0], sibling)
    ib[c, 1 - h, h] = xb[c, x, (y + 2) % 4]

    def pass_relay(p):
        here = relay.at[p]
        arrive(here, gr_s.at[p], gr_r.at[p])
        half = ((y + (3 if p % 2 == 0 else 1)) % 4) // 2
        n = quarter(p, 1 - half if p < 2 else half)
        send(here, gb.at[c, half, n], gy_s.at[p], gy_r.at[p], ring_y[2 * (p % 2)])

    pass_relay(0)
    pass_relay(1)

    low, high = pieces(c, xl, 0), pieces(c, xr, 1)
    arrive(low, x_s.at[0], x_r.at[0])
    send(low, low, x_s.at[4], x_r.at[4], right)
    arrive(high, x_s.at[1], x_r.at[1])
    send(high, high, x_s.at[5], x_r.at[5], left)
    pass_relay(2)
    pass_relay(3)

    def pass_gate(p):
        n = quarter(p, h if p < 2 else 1 - h)
        other = gb.at[c, 1 - h, n]
        arrive(other, gy_s.at[p], gy_r.at[p])
        send(other, other, gc_s.at[4 + p], gc_r.at[4 + p], sibling)

    def gate_passed(p):
        arrive(gb.at[1 - c, h, quarter(p, 1 - h if p < 2 else h)], gc_s.at[p], gc_r.at[p])
        arrive(gb.at[1 - c, 1 - h, quarter(p, h if p < 2 else 1 - h)], gc_s.at[4 + p], gc_r.at[4 + p])

    pass_gate(0)
    pass_gate(1)
    arrive(ib.at[c, 1 - h, 1 - h], y_s.at[0], y_r.at[0])
    send(ib.at[c], ib.at[c], cx_s.at[4], cx_r.at[4], sibling)
    arrive(ib.at[1 - c], cx_s.at[4], cx_r.at[4])

    def held_tile(t):
        slot = (t % 2) * 8 + t // 2
        held = jnp.int32(0)
        for k in range(16):
            held = jnp.maximum(held, jnp.where(owner_ref[0, k] == slot, k, 0))
        return held

    def partial_tile(t, slot):
        held = held_tile(t)
        px, py, pc = held >> 2, (held >> 1) & 1, held & 1
        total = jnp.zeros((160, 256), F32)
        for k in range(2):
            for m in range(2):
                total += jnp.dot(xb[k, px, 2 * m + py], gb[k, m, 2 * pc + c], preferred_element_type=F32)
        part[slot] = total

    def factor_rows(t):
        o_rows = pl.ds(pl.multiple_of(t * 32 + c * 16, 16), 16)
        i_rows = pl.ds(pl.multiple_of(t * 16, 16), 16)
        return jnp.concatenate(
            [osum[o_rows, k * 128:k * 128 + 128] for k in range(4)] + [isum[i_rows, :]], axis=0
        )


    def target(way, distance):
        return (z + distance) % Z if way == 0 else (z + Z - distance) % Z

    def place(index, way):
        return 0 if index == 0 else (index % 2) * 2 + way

    def own_part(stream, index, way):
        if stream == 0:
            return factor_rows(target(way, ORDER[index] if index < 8 else 0))
        return part[place(index, way), pl.ds(STREAM_FIRST[stream], STREAM_ROWS[stream])]

    def landed(stream, way, distance):
        came = ring[stream][0].at[way, distance - 1]
        arrive(came, rs_s.at[stream, way, distance - 1], rs_r.at[stream, way, distance - 1])
        return came[...].astype(F32)

    def hop(stream, index):
        distance = ORDER[index]
        for way in range(2):
            farthest = 8 if way == LONG_WAY[stream] else 7
            if distance > farthest:
                continue
            value = own_part(stream, index, way)
            if distance not in (farthest, REACH - 1):
                value = value + landed(stream, way, distance + 1)
            out = ring[stream][1].at[way, distance - 1]
            out[...] = value.astype(BF16)
            to = leap_z if distance == REACH else step_z
            send(out, ring[stream][0].at[way, distance - 1], rs_s.at[stream, way, distance - 1],
                 rs_r.at[stream, way, distance - 1], to[way])

    def finish(stream):
        value = own_part(stream, 8, 0)
        for distance in (1, REACH):
            for way in range(2):
                value = value + landed(stream, way, distance)
        return value * (1.0 / TOTAL)

    arrive(pieces(c, xl, 1), x_s.at[2], x_r.at[2])
    send(xb.at[c, xl], xb.at[c, xl], cx_s.at[1], cx_r.at[1], sibling)
    arrive(pieces(c, xr, 0), x_s.at[3], x_r.at[3])
    send(xb.at[c, xr], xb.at[c, xr], cx_s.at[2], cx_r.at[2], sibling)
    pass_gate(2)
    pass_gate(3)
    row = lax.broadcasted_iota(jnp.int32, (256, 160), 0)
    col = lax.broadcasted_iota(jnp.int32, (256, 160), 1)
    start = (row >> 4) * 10 + c * 5
    parts = []
    for b in range(3):
        at = (row & 15) - 5 * b
        parts.append(((col == start + at) & (at >= 0) & (at < 5)).astype(F32).astype(BF16))
    total = jnp.zeros((256, 128), F32)
    for k in range(2):
        for m in range(2):
            features = ib[k, m].reshape(320, 256)
            for b in range(3):
                rows = jnp.dot(parts[b], ib[k, m, h], preferred_element_type=F32).astype(BF16)
                columns = features[b * 128:min(b * 128 + 128, 320)]
                term = lax.dot_general(rows, columns, (((1,), (1,)), ((), ())), preferred_element_type=F32)
                if b == 2:
                    term = jnp.concatenate([term, jnp.zeros((256, 64), F32)], axis=1)
                total += term
    isum[...] = total

    for k in range(2):
        arrive(gb.at[1 - c, h, quarter(k, h)], gc_s.at[2 + k], gc_r.at[2 + k])
        arrive(gb.at[1 - c, 1 - h, quarter(k, h)], gc_s.at[4 + k], gc_r.at[4 + k])
    for i in range(2):
        for j in range(2):
            total = jnp.zeros((256, 256), F32)
            for k in range(2):
                for m in range(2):
                    total += lax.dot_general(
                        gb[k, m, 2 * h + i], gb[k, m, 2 * h + j],
                        (((0,), (0,)), ((), ())), preferred_element_type=F32,
                    )
            osum[pl.ds(i * 256, 256), pl.ds(j * 256, 256)] = total

    hop(0, 0)
    arrive(pieces(c, far, 0), x_s.at[4], x_r.at[4])
    arrive(pieces(c, far, 1), x_s.at[5], x_r.at[5])
    send(xb.at[c, far], xb.at[c, far], cx_s.at[3], cx_r.at[3], sibling)
    loads[5].wait()
    for k in range(2):
        arrive(gb.at[1 - c, h, quarter(k, 1 - h)], gc_s.at[k], gc_r.at[k])
        arrive(gb.at[1 - c, 1 - h, quarter(k, 1 - h)], gc_s.at[6 + k], gc_r.at[6 + k])
    for k, at in enumerate((x, xl, xr, far)):
        arrive(xb.at[1 - c, at], cx_s.at[k], cx_r.at[k])

    right_on = remote(rb, rb, r_s.at[1], r_r.at[1], across)

    for step in range(8):
        if step == 0:
            partial_tile(target(0, ORDER[0]), 0)
        ahead = [(step + 1, way) for way in range(2 if step < 7 else 1)]
        for k, stream in enumerate(TILE_STREAMS):
            hop(stream, step)
            if k % (len(TILE_STREAMS) // 2) == 0 and ahead:
                to, way = ahead.pop(0)
                partial_tile(target(way, ORDER[to] if to < 8 else 0), place(to, way))
        if step + LEAD < 8:
            hop(0, step + LEAD)
        if step == 0:
            @pl.when(home)
            def _():
                right_load.wait()
                arrive(right_slot(1 - zbit), r_s.at[0], r_r.at[0])
                right_on.start()
            loads[6].wait()
            lsplit[0], lsplit[1] = split(left_ref[...])
        if step == 5:
            pl.when(away)(right_on.wait_recv)
            rsplit[0], rsplit[1] = split(rb[...])
    for i in range(2):
        for stream in TILE_STREAMS:
            first = STREAM_FIRST[stream] - i * 80
            if 0 <= first < 80:
                piece[c, i, pl.ds(first, STREAM_ROWS[stream])] = finish(stream)
        mine = piece.at[c, i]
        send(mine, mine, p_s.at[i], p_r.at[i], sibling)
    factors = finish(0)
    for k in range(4):
        output_ref[:, k * 128:k * 128 + 128] = factors[k * 16:k * 16 + 16]
    for r in range(5):
        input_ref[r, :, 0:128] = factors[64 + r:65 + r]
        input_ref[r, :, 128:256] = factors[69 + r:70 + r]
        input_ref[r, :, 256:320] = factors[74 + r:75 + r, 0:64]

    goes = dev(x, zbit * 2 + ylo, zx, c)
    stay_copies = []
    for i in range(2):
        arrive(piece.at[1 - c, i], p_s.at[i], p_r.at[i])
        total = jnp.zeros((80, 256), F32)
        for k in range(2):
            rows = slice(k * 256, k * 256 + 256)
            total += dot3(split(piece[k, i]), (rsplit[0, rows], rsplit[1, rows]))
        rpart[0, i] = total[:, 0:128]
        rpart[1, i] = total[:, 128:256]
        send(rpart.at[1 - zbit, i], worker_part.at[h, i], d_s.at[i], d_r.at[h, i], goes)
        stay_copies.append(remote(rpart.at[zbit, i], worker_part.at[h, i], d_s.at[2 + i], d_r.at[h, i], across))
        pl.when(away)(stay_copies[i].start)

    @pl.when(home)
    def _():
        worker_part[h] = rpart[zbit]

    for i in range(2):
        @pl.when(away)
        def _():
            arrive(worker_part.at[h, i], d_s.at[i], d_r.at[h, i])
        arrive(worker_part.at[1 - h, i], d_s.at[i], d_r.at[1 - h, i])
    right_part = worker_part[...].reshape(320, 128)
    finished = dot3((lsplit[0], lsplit[1]), split(right_part))
    fin[...] = finished.reshape(320, 1, 128)

    def back_copy(to, at):
        return remote(fin.at[pl.ds(to * 5, 5)], ret.at[pl.ds(at * 5, 5)], t_s.at[to], t_r.at[at], (to, tn))

    def holder(off, k):
        return (k // 2) * 32 + lax.rem(z + off, Z) * 2 + k % 2

    def back(i, _):
        off = 8 + (i + 1) // 2 * (1 - 2 * (i % 2))
        for k in range(4):
            back_copy(holder(off, k), dp).start()
        return 0

    lax.fori_loop(0, 15, back, 0)
    for k in range(4):
        @pl.when(holder(0, k) != dp)
        def _():
            back_copy(holder(0, k), dp).start()
    ret[pl.ds(dp * 5, 5)] = fin[pl.ds(dp * 5, 5)]

    def back_wait(i, _):
        to = lax.rem(dp + i, 64)
        copy = back_copy(to, to)
        copy.wait_recv()
        copy.wait_send()
        return 0

    lax.fori_loop(1, 64, back_wait, 0)
    for a in range(8):
        for b in range(2):
            first = jnp.clip(owner_ref[0, a * 2 + b], 0, 15) * 20
            for w in range(4):
                at = b * 512 + w * 128
                pre_ref[:, a:a + 1, at:at + 128] = ret[pl.ds(first + w * 5, 5)]

    for copy in sends:
        copy.wait_send()

    @pl.when(home)
    def _():
        right_on.wait_send()

    @pl.when(away)
    def _():
        right_away.wait_send()
        for copy in stay_copies:
            copy.wait_send()


def store(a_in, b_in, c_in, a_out, b_out, c_out, a_mid, b_mid, c_mid, sems):
    ways = [(a_in, a_mid, a_out), (b_in, b_mid, b_out)]
    ways += [(c_in.at[r], c_mid.at[r], c_out.at[r]) for r in range(5)]
    fetches = [pltpu.make_async_copy(src, mid, sems.at[0, k]) for k, (src, mid, _) in enumerate(ways)]
    stores = [pltpu.make_async_copy(mid, dst, sems.at[1, k]) for k, (_, mid, dst) in enumerate(ways)]
    for copy in fetches:
        copy.start()
    for fetch, copy in zip(fetches, stores):
        fetch.wait()
        copy.start()
    for copy in stores:
        copy.wait()


def shards(inputs, gate_values, up_values, hidden_cotangent, owners, left_inverse, right_inverse):
    xt = inputs.T.reshape(2, 160, 256)
    vmem = pl.BlockSpec(memory_space=pltpu.VMEM)
    hbm = pl.BlockSpec(memory_space=pltpu.HBM)
    scratch = [
        pltpu.VMEM((3, 256, 1024), BF16),
        pltpu.SMEM((1, 16), jnp.int32),
        pltpu.VMEM((320, 320), F32),
        pltpu.VMEM((512, 256), F32),
        pltpu.VMEM((2, 512, 256), BF16),
        pltpu.VMEM((2, 320, 320), BF16),
        pltpu.VMEM((2, 4, 4, 160, 256), BF16),
        pltpu.VMEM((2, 2, 2, 160, 256), BF16),
        pltpu.VMEM((2, 2, 4, 256, 256), BF16),
        pltpu.VMEM((4, 256, 256), BF16),
        pltpu.VMEM((512, 512), F32),
        pltpu.VMEM((256, 128), F32),
        pltpu.VMEM((4, 160, 256), F32),
        pltpu.VMEM((2, 2, 80, 256), F32),
        pltpu.VMEM((2, 2, 80, 128), F32),
        pltpu.VMEM((2, 2, 80, 128), F32),
        pltpu.VMEM((320, 1, 128), F32),
        pltpu.VMEM((320, 1, 128), F32),
    ]
    scratch.append([
        [pltpu.VMEM((2, 8, rows, lanes), BF16)] * 2
        for rows, lanes in zip(STREAM_ROWS, STREAM_LANES)
    ])
    dma = pltpu.SemaphoreType.DMA
    for shape in ((8,), (4,), (4,), (6,), (6,), (5,), (5,), (4,), (4,), (4,), (4,), (8,), (8,), (2,), (2,),
                  (len(STREAM_ROWS), 2, 8), (len(STREAM_ROWS), 2, 8), (2,), (2,), (4,), (2, 2), (64,), (64,)):
        scratch.append(dma(shape))
    input_rows, output_rows, pre = pl.pallas_call(
        kernel,
        out_shape=(
            jax.ShapeDtypeStruct((5, 1, 320), F32),
            jax.ShapeDtypeStruct((16, 512), F32),
            jax.ShapeDtypeStruct((5, 8, 1024), F32),
        ),
        in_specs=[hbm] * 7,
        out_specs=(vmem, vmem, vmem),
        scratch_shapes=scratch,
        compiler_params=pltpu.CompilerParams(
            collective_id=0, has_side_effects=True, vmem_limit_bytes=62 * 2**20
        ),
        name="kfac",
    )(
        gate_values, up_values, hidden_cotangent, xt, left_inverse[0, 0], right_inverse[0, 0], owners,
    )
    results = (input_rows, output_rows, pre)
    input_rows, output_rows, pre = pl.pallas_call(
        store,
        out_shape=tuple(jax.ShapeDtypeStruct(r.shape, F32) for r in results),
        in_specs=[hbm] * 3,
        out_specs=(hbm,) * 3,
        scratch_shapes=[pltpu.VMEM(r.shape, F32) for r in results] + [dma((2, 7))],
        compiler_params=pltpu.CompilerParams(vmem_limit_bytes=62 * 2**20),
        name="store",
    )(*results)
    return input_rows.transpose(1, 0, 2), output_rows[None], pre.transpose(1, 0, 2)


def solution(mesh):
    in_specs = (
        P("dp", "tensor"), P("dp", "tensor"), P("dp", "tensor"), P("dp", "tensor"), P("tensor", None),
        P("dp", "tensor", None, None), P("dp", "tensor", None, None),
    )
    out_specs = (P("tensor", "dp", None), P("tensor", "dp", None), P(None, "dp", "tensor"))
    return jax.shard_map(shards, mesh=mesh, in_specs=in_specs, out_specs=out_specs, check_vma=False)
```

```python
import jax
import jax.numpy as jnp
from jax import lax
from jax.experimental import pallas as pl
from jax.experimental.pallas import tpu as pltpu
from jax.sharding import PartitionSpec as P

MESH = pl.DeviceIdType.MESH
F32 = jnp.float32
BF16 = jnp.bfloat16
Z = 16
REACH = 4
ORDER = (8, 7, 6, 3, 5, 2, 4, 1)
TOTAL = 16384
LEAD = 1
STREAM_ROWS = (80, 80, 80)
STREAM_FIRST = (0, 0, 80)
STREAM_LANES = (128, 256, 256)
LONG_WAY = (0, 0, 1)
TILE_STREAMS = tuple(range(1, len(STREAM_ROWS)))


def split(value):
    high = value.astype(BF16)
    return high, (value - high.astype(F32)).astype(BF16)


def dot3(a, b):
    (a_hi, a_lo), (b_hi, b_lo) = a, b
    total = jnp.dot(a_hi, b_hi, preferred_element_type=F32)
    total += jnp.dot(a_hi, b_lo, preferred_element_type=F32)
    return total + jnp.dot(a_lo, b_hi, preferred_element_type=F32)


def kernel(
    gate_in, up_in, cot_in, xt_in, left_in, right_in, owner_in,
    input_ref, output_ref, pre_ref,
    gates, owner_ref, left_ref, rb, rsplit, lsplit,
    xb, ib, gb, relay, osum, isum, part, piece, rpart, worker_part, fin, ret,
    ring,
    l_s, y_s, y_r, x_s, x_r, cx_s, cx_r, gr_s, gr_r, gy_s, gy_r, gc_s, gc_r, r_s, r_r,
    rs_s, rs_r, p_s, p_r, d_s, d_r, t_s, t_r,
):
    dp = lax.axis_index("dp")
    tn = lax.axis_index("tensor")
    h, z, c = dp // 32, (dp // 2) % Z, dp % 2
    x, ylo = tn // 2, tn % 2
    y = h * 2 + ylo
    zbit = z % 2
    home = h == zbit
    away = jnp.logical_not(home)

    def dev(x_, y_, z_, c_):
        return ((y_ // 2) * 32 + z_ * 2 + c_, x_ * 2 + y_ % 2)

    xr, xl, far = (x + 1) % 4, (x + 3) % 4, (x + 2) % 4
    zx = z + 1 - 2 * zbit
    sibling = dev(x, y, z, 1 - c)
    across = dev(x, (y + 2) % 4, z, c)
    right, left = dev(xr, y, z, c), dev(xl, y, z, c)
    step_z = (dev(x, y, (z + 1) % Z, c), dev(x, y, (z + Z - 1) % Z, c))
    leap_z = (dev(x, y, (z + REACH) % Z, c), dev(x, y, (z + Z - REACH) % Z, c))
    pair_z = dev(x, y, zx, c)
    diagonal = dev(x, (y + 2) % 4, zx, c)
    ring_y = [dev(x, (y + k) % 4, z, c) for k in (1, 2, 3)]

    barrier = pltpu.get_barrier_semaphore()
    peers = ring_y + [right, left, sibling, diagonal, *step_z, *leap_z]
    for peer in peers:
        pl.semaphore_signal(barrier, inc=1, device_id=peer, device_id_type=MESH)

    loads = [
        pltpu.make_async_copy(src, dst, l_s.at[k])
        for k, (src, dst) in enumerate((
            (xt_in.at[h], xb.at[c, x, y]), (xt_in, ib.at[c, h]),
            (gate_in, gates.at[0]), (up_in, gates.at[1]), (cot_in, gates.at[2]),
            (owner_in, owner_ref), (left_in, left_ref),
        ))
    ]
    for load in loads:
        load.start()

    def right_slot(which):
        return rb.at[:, pl.ds(pl.multiple_of(which * 128, 128), 128)]

    right_load = pltpu.make_async_copy(right_in, right_slot(zbit), l_s.at[7])
    pl.when(home)(right_load.start)
    pl.semaphore_wait(barrier, len(peers))

    sends = []

    def remote(src, dst, s_sem, r_sem, to):
        return pltpu.make_async_remote_copy(
            src_ref=src, dst_ref=dst, send_sem=s_sem, recv_sem=r_sem, device_id=to, device_id_type=MESH
        )

    def send(src, dst, s_sem, r_sem, to):
        copy = remote(src, dst, s_sem, r_sem, to)
        copy.start()
        sends.append(copy)

    def arrive(dst, s_sem, r_sem):
        remote(dst, dst, s_sem, r_sem, sibling).wait_recv()

    for k in (1, 3, 2):
        half = ((y + k) % 4) // 2
        send(xt_in.at[half], xb.at[c, x, y], y_s.at[k], y_r.at[k], ring_y[k - 1])
    right_away = remote(right_in, right_slot(zbit), r_s.at[0], r_r.at[0], pair_z)
    pl.when(away)(right_away.start)

    def quarter(p, block):
        return 2 * block + p % 2

    for load in loads[2:5]:
        load.wait()
    for p in range(4):
        n = quarter(p, 1 - h if p < 2 else h)
        cols = pl.ds(pl.multiple_of(n * 256, 256), 256)
        pre = gates[0, :, cols].astype(F32)
        s = jax.nn.sigmoid(pre)
        slope = s * (1.0 + pre * (1.0 - s))
        gb[c, h, n] = (gates[2, :, cols].astype(F32) * gates[1, :, cols].astype(F32) * slope).astype(BF16)
        mine = gb.at[c, h, n]
        send(mine, relay.at[p], gr_s.at[p], gr_r.at[p], ring_y[2 * (p % 2)])
        send(mine, mine, gc_s.at[p], gc_r.at[p], sibling)
        if p == 1:
            send(xt_in.at[h], ib.at[c, h, h], y_s.at[0], y_r.at[0], across)
    loads[0].wait()
    loads[1].wait()

    for k in (1, 3, 2):
        arrive(xb.at[c, x, (y + 4 - k) % 4], y_s.at[k], y_r.at[k])

    def pieces(core, place, k):
        return xb.at[core, place, pl.ds(2 * k, 2)]

    own = (pieces(c, x, 0), pieces(c, x, 1))
    send(own[0], own[0], x_s.at[0], x_r.at[0], right)
    send(own[1], own[1], x_s.at[1], x_r.at[1], left)
    send(own[1], own[1], x_s.at[2], x_r.at[2], right)
    send(own[0], own[0], x_s.at[3], x_r.at[3], left)
    send(xb.at[c, x], xb.at[c, x], cx_s.at[0], cx_r.at[0], sibling)
    ib[c, 1 - h, h] = xb[c, x, (y + 2) % 4]

    def pass_relay(p):
        here = relay.at[p]
        arrive(here, gr_s.at[p], gr_r.at[p])
        half = ((y + (3 if p % 2 == 0 else 1)) % 4) // 2
        n = quarter(p, 1 - half if p < 2 else half)
        send(here, gb.at[c, half, n], gy_s.at[p], gy_r.at[p], ring_y[2 * (p % 2)])

    pass_relay(0)
    pass_relay(1)

    low, high = pieces(c, xl, 0), pieces(c, xr, 1)
    arrive(low, x_s.at[0], x_r.at[0])
    send(low, low, x_s.at[4], x_r.at[4], right)
    arrive(high, x_s.at[1], x_r.at[1])
    send(high, high, x_s.at[5], x_r.at[5], left)
    pass_relay(2)
    pass_relay(3)

    def pass_gate(p):
        n = quarter(p, h if p < 2 else 1 - h)
        other = gb.at[c, 1 - h, n]
        arrive(other, gy_s.at[p], gy_r.at[p])
        send(other, other, gc_s.at[4 + p], gc_r.at[4 + p], sibling)

    def gate_passed(p):
        arrive(gb.at[1 - c, h, quarter(p, 1 - h if p < 2 else h)], gc_s.at[p], gc_r.at[p])
        arrive(gb.at[1 - c, 1 - h, quarter(p, h if p < 2 else 1 - h)], gc_s.at[4 + p], gc_r.at[4 + p])

    pass_gate(0)
    pass_gate(1)
    arrive(ib.at[c, 1 - h, 1 - h], y_s.at[0], y_r.at[0])
    send(ib.at[c], ib.at[c], cx_s.at[4], cx_r.at[4], sibling)
    arrive(ib.at[1 - c], cx_s.at[4], cx_r.at[4])

    def held_tile(t):
        slot = (t % 2) * 8 + t // 2
        held = jnp.int32(0)
        for k in range(16):
            held = jnp.maximum(held, jnp.where(owner_ref[0, k] == slot, k, 0))
        return held

    def partial_tile(t, slot):
        held = held_tile(t)
        px, py, pc = held >> 2, (held >> 1) & 1, held & 1
        total = jnp.zeros((160, 256), F32)
        for k in range(2):
            for m in range(2):
                total += jnp.dot(xb[k, px, 2 * m + py], gb[k, m, 2 * pc + c], preferred_element_type=F32)
        part[slot] = total

    def factor_rows(t):
        o_rows = pl.ds(pl.multiple_of(t * 32 + c * 16, 16), 16)
        i_rows = pl.ds(pl.multiple_of(t * 16, 16), 16)
        return jnp.concatenate(
            [osum[o_rows, k * 128:k * 128 + 128] for k in range(4)] + [isum[i_rows, :]], axis=0
        )


    def target(way, distance):
        return (z + distance) % Z if way == 0 else (z + Z - distance) % Z

    def place(index, way):
        return 0 if index == 0 else (index % 2) * 2 + way

    def own_part(stream, index, way):
        if stream == 0:
            return factor_rows(target(way, ORDER[index] if index < 8 else 0))
        return part[place(index, way), pl.ds(STREAM_FIRST[stream], STREAM_ROWS[stream])]

    def landed(stream, way, distance):
        came = ring[stream][0].at[way, distance - 1]
        arrive(came, rs_s.at[stream, way, distance - 1], rs_r.at[stream, way, distance - 1])
        return came[...].astype(F32)

    def hop(stream, index):
        distance = ORDER[index]
        for way in range(2):
            farthest = 8 if way == LONG_WAY[stream] else 7
            if distance > farthest:
                continue
            value = own_part(stream, index, way)
            if distance not in (farthest, REACH - 1):
                value = value + landed(stream, way, distance + 1)
            out = ring[stream][1].at[way, distance - 1]
            out[...] = value.astype(BF16)
            to = leap_z if distance == REACH else step_z
            send(out, ring[stream][0].at[way, distance - 1], rs_s.at[stream, way, distance - 1],
                 rs_r.at[stream, way, distance - 1], to[way])

    def finish(stream):
        value = own_part(stream, 8, 0)
        for distance in (1, REACH):
            for way in range(2):
                value = value + landed(stream, way, distance)
        return value * (1.0 / TOTAL)

    arrive(pieces(c, xl, 1), x_s.at[2], x_r.at[2])
    send(xb.at[c, xl], xb.at[c, xl], cx_s.at[1], cx_r.at[1], sibling)
    arrive(pieces(c, xr, 0), x_s.at[3], x_r.at[3])
    send(xb.at[c, xr], xb.at[c, xr], cx_s.at[2], cx_r.at[2], sibling)
    pass_gate(2)
    pass_gate(3)
    row = lax.broadcasted_iota(jnp.int32, (256, 160), 0)
    col = lax.broadcasted_iota(jnp.int32, (256, 160), 1)
    start = (row >> 4) * 10 + c * 5
    parts = []
    for b in range(3):
        at = (row & 15) - 5 * b
        parts.append(((col == start + at) & (at >= 0) & (at < 5)).astype(F32).astype(BF16))
    total = jnp.zeros((256, 128), F32)
    for k in range(2):
        for m in range(2):
            features = ib[k, m].reshape(320, 256)
            for b in range(3):
                rows = jnp.dot(parts[b], ib[k, m, h], preferred_element_type=F32).astype(BF16)
                columns = features[b * 128:min(b * 128 + 128, 320)]
                term = lax.dot_general(rows, columns, (((1,), (1,)), ((), ())), preferred_element_type=F32)
                if b == 2:
                    term = jnp.concatenate([term, jnp.zeros((256, 64), F32)], axis=1)
                total += term
    isum[...] = total

    for k in range(2):
        arrive(gb.at[1 - c, h, quarter(k, h)], gc_s.at[2 + k], gc_r.at[2 + k])
        arrive(gb.at[1 - c, 1 - h, quarter(k, h)], gc_s.at[4 + k], gc_r.at[4 + k])
    for i in range(2):
        for j in range(2):
            total = jnp.zeros((256, 256), F32)
            for k in range(2):
                for m in range(2):
                    total += lax.dot_general(
                        gb[k, m, 2 * h + i], gb[k, m, 2 * h + j],
                        (((0,), (0,)), ((), ())), preferred_element_type=F32,
                    )
            osum[pl.ds(i * 256, 256), pl.ds(j * 256, 256)] = total

    hop(0, 0)
    arrive(pieces(c, far, 0), x_s.at[4], x_r.at[4])
    arrive(pieces(c, far, 1), x_s.at[5], x_r.at[5])
    send(xb.at[c, far], xb.at[c, far], cx_s.at[3], cx_r.at[3], sibling)
    loads[5].wait()
    for k in range(2):
        arrive(gb.at[1 - c, h, quarter(k, 1 - h)], gc_s.at[k], gc_r.at[k])
        arrive(gb.at[1 - c, 1 - h, quarter(k, 1 - h)], gc_s.at[6 + k], gc_r.at[6 + k])
    for k, at in enumerate((x, xl, xr, far)):
        arrive(xb.at[1 - c, at], cx_s.at[k], cx_r.at[k])

    right_on = remote(rb, rb, r_s.at[1], r_r.at[1], across)

    for step in range(8):
        if step == 0:
            partial_tile(target(0, ORDER[0]), 0)
        ahead = [(step + 1, way) for way in range(2 if step < 7 else 1)]
        for k, stream in enumerate(TILE_STREAMS):
            hop(stream, step)
            if k % (len(TILE_STREAMS) // 2) == 0 and ahead:
                to, way = ahead.pop(0)
                partial_tile(target(way, ORDER[to] if to < 8 else 0), place(to, way))
        if step + LEAD < 8:
            hop(0, step + LEAD)
        if step == 0:
            @pl.when(home)
            def _():
                right_load.wait()
                arrive(right_slot(1 - zbit), r_s.at[0], r_r.at[0])
                right_on.start()
            loads[6].wait()
            lsplit[0], lsplit[1] = split(left_ref[...])
        if step == 5:
            pl.when(away)(right_on.wait_recv)
            rsplit[0], rsplit[1] = split(rb[...])
    for i in range(2):
        for stream in TILE_STREAMS:
            first = STREAM_FIRST[stream] - i * 80
            if 0 <= first < 80:
                piece[c, i, pl.ds(first, STREAM_ROWS[stream])] = finish(stream)
        mine = piece.at[c, i]
        send(mine, mine, p_s.at[i], p_r.at[i], sibling)
    def product(core, i):
        rows = pl.ds(pl.multiple_of(core * 256, 256), 256)
        return dot3(split(piece[core, i]), (rsplit[0, rows], rsplit[1, rows]))

    own_products = [product(c, 0), product(c, 1)]
    factors = finish(0)
    for k in range(4):
        output_ref[:, k * 128:k * 128 + 128] = factors[k * 16:k * 16 + 16]
    for r in range(5):
        input_ref[r, :, 0:128] = factors[64 + r:65 + r]
        input_ref[r, :, 128:256] = factors[69 + r:70 + r]
        input_ref[r, :, 256:320] = factors[74 + r:75 + r, 0:64]

    goes = dev(x, zbit * 2 + ylo, zx, c)
    stay_copies = []
    for i in range(2):
        arrive(piece.at[1 - c, i], p_s.at[i], p_r.at[i])
        total = own_products[i] + product(1 - c, i)
        rpart[0, i] = total[:, 0:128]
        rpart[1, i] = total[:, 128:256]
        send(rpart.at[1 - zbit, i], worker_part.at[h, i], d_s.at[i], d_r.at[h, i], goes)
        stay_copies.append(remote(rpart.at[zbit, i], worker_part.at[h, i], d_s.at[2 + i], d_r.at[h, i], across))
        pl.when(away)(stay_copies[i].start)

    @pl.when(home)
    def _():
        worker_part[h] = rpart[zbit]

    for i in range(2):
        @pl.when(away)
        def _():
            arrive(worker_part.at[h, i], d_s.at[i], d_r.at[h, i])
        arrive(worker_part.at[1 - h, i], d_s.at[i], d_r.at[1 - h, i])
    right_part = worker_part[...].reshape(320, 128)
    finished = dot3((lsplit[0], lsplit[1]), split(right_part))
    fin[...] = finished.reshape(320, 1, 128)

    def back_copy(to, at):
        return remote(fin.at[pl.ds(to * 5, 5)], ret.at[pl.ds(at * 5, 5)], t_s.at[to], t_r.at[at], (to, tn))

    def holder(off, k):
        return (k // 2) * 32 + lax.rem(z + off, Z) * 2 + k % 2

    def back(i, _):
        off = 8 + (i + 1) // 2 * (1 - 2 * (i % 2))
        for k in range(4):
            back_copy(holder(off, k), dp).start()
        return 0

    lax.fori_loop(0, 15, back, 0)
    for k in range(4):
        @pl.when(holder(0, k) != dp)
        def _():
            back_copy(holder(0, k), dp).start()
    ret[pl.ds(dp * 5, 5)] = fin[pl.ds(dp * 5, 5)]

    def back_wait(i, _):
        to = lax.rem(dp + i, 64)
        copy = back_copy(to, to)
        copy.wait_recv()
        copy.wait_send()
        return 0

    lax.fori_loop(1, 64, back_wait, 0)
    for a in range(8):
        for b in range(2):
            first = jnp.clip(owner_ref[0, a * 2 + b], 0, 15) * 20
            for w in range(4):
                at = b * 512 + w * 128
                pre_ref[:, a:a + 1, at:at + 128] = ret[pl.ds(first + w * 5, 5)]

    for copy in sends:
        copy.wait_send()

    @pl.when(home)
    def _():
        right_on.wait_send()

    @pl.when(away)
    def _():
        right_away.wait_send()
        for copy in stay_copies:
            copy.wait_send()


def store(a_in, b_in, c_in, a_out, b_out, c_out, a_mid, b_mid, c_mid, sems):
    ways = [(a_in, a_mid, a_out), (b_in, b_mid, b_out)]
    ways += [(c_in.at[r], c_mid.at[r], c_out.at[r]) for r in range(5)]
    fetches = [pltpu.make_async_copy(src, mid, sems.at[0, k]) for k, (src, mid, _) in enumerate(ways)]
    stores = [pltpu.make_async_copy(mid, dst, sems.at[1, k]) for k, (_, mid, dst) in enumerate(ways)]
    for copy in fetches:
        copy.start()
    for fetch, copy in zip(fetches, stores):
        fetch.wait()
        copy.start()
    for copy in stores:
        copy.wait()


def shards(inputs, gate_values, up_values, hidden_cotangent, owners, left_inverse, right_inverse):
    xt = inputs.T.reshape(2, 160, 256)
    vmem = pl.BlockSpec(memory_space=pltpu.VMEM)
    hbm = pl.BlockSpec(memory_space=pltpu.HBM)
    scratch = [
        pltpu.VMEM((3, 256, 1024), BF16),
        pltpu.SMEM((1, 16), jnp.int32),
        pltpu.VMEM((320, 320), F32),
        pltpu.VMEM((512, 256), F32),
        pltpu.VMEM((2, 512, 256), BF16),
        pltpu.VMEM((2, 320, 320), BF16),
        pltpu.VMEM((2, 4, 4, 160, 256), BF16),
        pltpu.VMEM((2, 2, 2, 160, 256), BF16),
        pltpu.VMEM((2, 2, 4, 256, 256), BF16),
        pltpu.VMEM((4, 256, 256), BF16),
        pltpu.VMEM((512, 512), F32),
        pltpu.VMEM((256, 128), F32),
        pltpu.VMEM((4, 160, 256), F32),
        pltpu.VMEM((2, 2, 80, 256), F32),
        pltpu.VMEM((2, 2, 80, 128), F32),
        pltpu.VMEM((2, 2, 80, 128), F32),
        pltpu.VMEM((320, 1, 128), F32),
        pltpu.VMEM((320, 1, 128), F32),
    ]
    scratch.append([
        [pltpu.VMEM((2, 8, rows, lanes), BF16)] * 2
        for rows, lanes in zip(STREAM_ROWS, STREAM_LANES)
    ])
    dma = pltpu.SemaphoreType.DMA
    for shape in ((8,), (4,), (4,), (6,), (6,), (5,), (5,), (4,), (4,), (4,), (4,), (8,), (8,), (2,), (2,),
                  (len(STREAM_ROWS), 2, 8), (len(STREAM_ROWS), 2, 8), (2,), (2,), (4,), (2, 2), (64,), (64,)):
        scratch.append(dma(shape))
    input_rows, output_rows, pre = pl.pallas_call(
        kernel,
        out_shape=(
            jax.ShapeDtypeStruct((5, 1, 320), F32),
            jax.ShapeDtypeStruct((16, 512), F32),
            jax.ShapeDtypeStruct((5, 8, 1024), F32),
        ),
        in_specs=[hbm] * 7,
        out_specs=(vmem, vmem, vmem),
        scratch_shapes=scratch,
        compiler_params=pltpu.CompilerParams(
            collective_id=0, has_side_effects=True, vmem_limit_bytes=62 * 2**20
        ),
        name="kfac",
    )(
        gate_values, up_values, hidden_cotangent, xt, left_inverse[0, 0], right_inverse[0, 0], owners,
    )
    results = (input_rows, output_rows, pre)
    input_rows, output_rows, pre = pl.pallas_call(
        store,
        out_shape=tuple(jax.ShapeDtypeStruct(r.shape, F32) for r in results),
        in_specs=[hbm] * 3,
        out_specs=(hbm,) * 3,
        scratch_shapes=[pltpu.VMEM(r.shape, F32) for r in results] + [dma((2, 7))],
        compiler_params=pltpu.CompilerParams(vmem_limit_bytes=62 * 2**20),
        name="store",
    )(*results)
    return input_rows.transpose(1, 0, 2), output_rows[None], pre.transpose(1, 0, 2)


def solution(mesh):
    in_specs = (
        P("dp", "tensor"), P("dp", "tensor"), P("dp", "tensor"), P("dp", "tensor"), P("tensor", None),
        P("dp", "tensor", None, None), P("dp", "tensor", None, None),
    )
    out_specs = (P("tensor", "dp", None), P("tensor", "dp", None), P(None, "dp", "tensor"))
    return jax.shard_map(shards, mesh=mesh, in_specs=in_specs, out_specs=out_specs, check_vma=False)
```
